256 devices in a mesh: center: 64 (over y, z, core), rep: 4 (over x).
Axes of the slice: x: 4, y: 4, z: 8, core: 2. Of those that a mesh axis runs over, the one named last changes fastest.
Arguments:
- faces: bfloat16 [16384, 512], P(('center', 'rep')), may hold values from -1800 to 1800
- w_first: bfloat16 [512, 512], replicated, may hold values from -1.1 to 1.1
- w_second: bfloat16 [512, 512], replicated, may hold values from -1.1 to 1.1
- gain_first: float32 [512], replicated, may hold values from 0.46 to 1.54
- bias_first: float32 [512], replicated, may hold values from -3 to 3
- gain_second: float32 [512], replicated, may hold values from 0.46 to 1.54
- centers: float32 [131072, 512], P('center'), may hold values from -6 to 6
- momentum: float32 [131072, 512], P('center'), may hold values from -1.2 to 1.2
- sample_index: int32 [8192], P('center'), may hold values from 0 to 2047, as said below
- live_count: int32 [64], P('center'), may hold values from 16 to 128, as said below
- labels: int32 [16384], P(('center', 'rep')), may hold values from 0 to 8191, as said below
Outputs:
- loss: float32 [16384], P(('center', 'rep'))
- feat_grad: float32 [16384, 512], P(('center', 'rep'))
- new_centers: float32 [8192, 512], P('center')
- new_momentum: float32 [8192, 512], P('center')
The draws below stay inside these ranges and needn't reach their ends.
Inputs may be any that keep to these rules, and one draw needn't show every extreme that they name: `sample_index`: the 128 entries of one shard are distinct rows of that shard. The live slots of a shard are its first live_count entries; some shard has 128 of them and some shard 128 // 8. `labels`: each label is a live sampled slot, counted over all shards' lists in shard order.
All inputs are finite; a program needn't handle non-finite values.
Results may differ from the reference program's by a relative error of at most 0.0075.
Values may be sent and summed in bfloat16 or wider, within the bound.
A program may use at most 64 MiB of HBM per device.

```python
import math
import jax
import jax.numpy as jnp
from jax import lax

D = 512
FACE_DEV = 64
ROWS_DEV = 2048
SAMP = 128
SHARDS = 64
REPS = 4
FACES = 16384
CENTERS = 131072
SAMPLED = 8192


def head_params(key):
    subkeys = jax.random.split(jax.random.fold_in(key, 3), 5)
    scale_in = 1.0 / math.sqrt(D)
    w_first = jnp.clip(jax.random.normal(subkeys[0], (D, D), jnp.float32), -6.0, 6.0) * scale_in
    w_second = jnp.clip(jax.random.normal(subkeys[1], (D, D), jnp.float32), -6.0, 6.0) * scale_in
    gain_first = 1.0 + 0.18 * jnp.clip(jax.random.normal(subkeys[2], (D,), jnp.float32), -3.0, 3.0)
    bias_first = 0.5 * jnp.clip(jax.random.normal(subkeys[3], (D,), jnp.float32), -6.0, 6.0)
    gain_second = 1.0 + 0.18 * jnp.clip(jax.random.normal(subkeys[4], (D,), jnp.float32), -3.0, 3.0)
    return (w_first, w_second, gain_first, bias_first, gain_second)


def draw_w_first(key, part):
    return head_params(key)[0].astype(jnp.bfloat16)


def draw_w_second(key, part):
    return head_params(key)[1].astype(jnp.bfloat16)


def draw_gain_first(key, part):
    return head_params(key)[2]


def draw_bias_first(key, part):
    return head_params(key)[3]


def draw_gain_second(key, part):
    return head_params(key)[4]


def draw_sample_index(key, part):
    shard_keys = jax.random.split(jax.random.fold_in(key, 11), SHARDS)

    def one_shard(shard_key):
        return jax.random.permutation(shard_key, ROWS_DEV)[:SAMP]
    chosen = jax.vmap(one_shard)(shard_keys)
    return chosen.reshape(SHARDS * SAMP).astype(jnp.int32)


def live_and_labels(key):
    base_key = jax.random.fold_in(key, 7)
    key_count, key_full, key_low, key_owner, key_slot = jax.random.split(base_key, 5)
    counts = jax.random.randint(key_count, (SHARDS,), SAMP // 8, SAMP + 1)
    full_shard = jax.random.randint(key_full, (), 0, SHARDS)
    low_shard = (full_shard + 1 + jax.random.randint(key_low, (), 0, SHARDS - 1)) % SHARDS
    counts = counts.at[low_shard].set(SAMP // 8).at[full_shard].set(SAMP)
    owners = jax.random.randint(key_owner, (FACES,), 0, SHARDS)
    slot_draw = jax.random.randint(key_slot, (FACES,), 0, 1 << 20) % counts[owners]
    label_vals = owners * SAMP + slot_draw
    return (counts.astype(jnp.int32), label_vals.astype(jnp.int32))


def draw_live_count(key, part):
    return live_and_labels(key)[0]


def draw_labels(key, part):
    return live_and_labels(key)[1]


def face_values(key):
    key_rows, key_cols, key_base = jax.random.split(key, 3)
    block_ids = jnp.arange(FACES) // FACE_DEV
    rising = 1.0 + 2.0 * (block_ids % REPS).astype(jnp.float32) / max(REPS - 1, 1)
    col_scale = jnp.exp(jax.random.uniform(key_cols, (1, D), jnp.float32, 0.0, math.log(10.0)))
    row_scale = jnp.exp(jax.random.uniform(key_rows, (FACES, 1), jnp.float32, 0.0, math.log(10.0)))
    base_vals = jnp.clip(jax.random.normal(key_base, (FACES, D), jnp.float32), -6.0, 6.0)
    return base_vals * row_scale * col_scale * rising[:, None]


def draw_faces(key, part):
    return face_values(key).astype(jnp.bfloat16)


def draw_centers(key, part):
    key_noise = jax.random.fold_in(jax.random.fold_in(key, 17), 1)
    noise = jnp.clip(jax.random.normal(key_noise, (CENTERS, D), jnp.float32), -6.0, 6.0)
    values = noise
    return jnp.clip(values, -6.0, 6.0)


def steps_of(own_key, dims, cuts, smallest, top_value):
    loudness = 1.0
    for axis_at, parts in cuts:
        draws = jax.random.uniform(jax.random.fold_in(jax.random.fold_in(own_key, 6), axis_at), (parts,), jnp.float32, smallest / len(cuts), top_value / len(cuts))
        loudness = loudness * jnp.repeat(jnp.exp(draws), dims[axis_at] // parts).reshape((-1,) + (1,) * (len(dims) - 1 - axis_at))
    return loudness


def gaussian(stream_key, dims, scale, bound, cuts=(), held_as=jnp.bfloat16):
    array = jax.random.normal(stream_key, dims, jnp.float32) * scale
    if len(cuts) > 0:
        array = steps_of(stream_key, dims, cuts, -0.22, 0.18) * array
    return jnp.clip(array, min=-bound, max=bound).astype(held_as)


def setup_inputs(seed: int = 0) -> dict:
    splits = jax.random.split(jax.random.key(seed), 12)
    faces = draw_faces(jax.random.fold_in(splits[11], 71), 0)
    w_first = draw_w_first(jax.random.fold_in(splits[11], 71), 0)
    w_second = draw_w_second(jax.random.fold_in(splits[11], 71), 0)
    gain_first = draw_gain_first(jax.random.fold_in(splits[11], 71), 0)
    bias_first = draw_bias_first(jax.random.fold_in(splits[11], 71), 0)
    gain_second = draw_gain_second(jax.random.fold_in(splits[11], 71), 0)
    centers = draw_centers(jax.random.fold_in(splits[11], 71), 0)
    momentum = gaussian(splits[7], (CENTERS, D), 0.2, 1.2, ((0, 64),), jnp.float32)
    sample_index = draw_sample_index(jax.random.fold_in(splits[11], 71), 0)
    live_count = draw_live_count(jax.random.fold_in(splits[11], 71), 0)
    labels = draw_labels(jax.random.fold_in(splits[11], 71), 0)
    return dict(faces=faces, w_first=w_first, w_second=w_second, gain_first=gain_first, bias_first=bias_first, gain_second=gain_second, centers=centers, momentum=momentum, sample_index=sample_index, live_count=live_count, labels=labels)


LOGIT_SCALE = 64.0
COS_MARGIN = 0.35
LEARN_RATE = 0.5
MOMENT_COEF = 0.9
DECAY_COEF = 0.0005
NORM_EPS = 1e-05
LENGTH_EPS = 1e-06

def normalize_batch(values, gain_vec):
    grouped = values.reshape(-1, FACE_DEV * REPS, values.shape[1])
    mean_vec = lax.optimization_barrier(jnp.mean(grouped, 1, keepdims=True))
    centered = grouped - mean_vec
    spread = lax.optimization_barrier(jnp.mean(centered * centered, 1, keepdims=True))
    return (gain_vec * centered * lax.rsqrt(spread + NORM_EPS)).reshape(values.shape)

def reference(faces, w_first, w_second, gain_first, bias_first, gain_second, centers, momentum, sample_index, live_count, labels):
    first_out = jnp.dot(faces, w_first, preferred_element_type=jnp.float32)
    hidden = jnp.maximum(normalize_batch(first_out, gain_first) + bias_first, 0.0).astype(jnp.bfloat16)
    second = jnp.dot(hidden, w_second, preferred_element_type=jnp.float32)
    feature = normalize_batch(second, gain_second)
    length = jnp.sqrt(lax.optimization_barrier(jnp.sum(feature * feature, 1, keepdims=True)) + LENGTH_EPS)
    unit_rows = feature / length
    unit_low = unit_rows.astype(jnp.bfloat16)
    slot_ids = jnp.arange(SAMPLED).astype(jnp.int32)
    owner = (slot_ids // SAMP).astype(jnp.int32)
    table_rows = (owner * ROWS_DEV + sample_index).astype(jnp.int32)
    picked = jnp.take(centers, table_rows, axis=0)
    picked_momentum = jnp.take(momentum, table_rows, axis=0)
    center_len = jnp.sqrt(lax.optimization_barrier(jnp.sum(picked * picked, 1, keepdims=True)) + LENGTH_EPS)
    center_unit = picked / center_len
    center_low = center_unit.astype(jnp.bfloat16)
    live_slot = slot_ids % SAMP < jnp.take(live_count, owner)
    block_rows = min(1024, FACES)
    unit_blocks = unit_low.reshape(FACES // block_rows, block_rows, D)
    label_blocks = labels.reshape(FACES // block_rows, block_rows)

    def score_block(running, element):
        unit_block, mark_block = element
        cosine = jnp.dot(unit_block, center_low.T, preferred_element_type=jnp.float32)
        target = mark_block[:, None] == slot_ids[None, :]
        logits = LOGIT_SCALE * (cosine - COS_MARGIN * target.astype(jnp.float32))
        exponent = jnp.where(live_slot[None, :], jnp.exp(logits), 0.0)
        softmax_total = lax.optimization_barrier(jnp.sum(exponent, 1))
        target_logit = lax.optimization_barrier(jnp.sum(jnp.where(target, logits, 0.0), 1))
        face_loss = jnp.log(softmax_total) - target_logit
        weight = (LOGIT_SCALE * (exponent / softmax_total[:, None] - target.astype(jnp.float32))).astype(jnp.bfloat16)
        unit_grad = jnp.dot(weight, center_low, preferred_element_type=jnp.float32)
        running = running + jnp.dot(weight.T, unit_block, preferred_element_type=jnp.float32)
        return (running, (face_loss, unit_grad))
    start_sum = jnp.zeros((SAMPLED, D), jnp.float32)
    center_raw, (loss_blocks, grad_blocks) = lax.scan(score_block, start_sum, (unit_blocks, label_blocks))
    loss = loss_blocks.reshape(FACES)
    unit_grad = grad_blocks.reshape(FACES, D)
    radial = lax.optimization_barrier(jnp.sum(unit_rows * unit_grad, 1, keepdims=True))
    feat_grad = (unit_grad - unit_rows * radial) / length
    center_radial = lax.optimization_barrier(jnp.sum(center_unit * center_raw, 1, keepdims=True))
    center_grad = (center_raw - center_unit * center_radial) / center_len
    velocity = MOMENT_COEF * picked_momentum + center_grad + DECAY_COEF * picked
    new_momentum = jnp.where(live_slot[:, None], velocity, picked_momentum)
    new_centers = jnp.where(live_slot[:, None], picked - LEARN_RATE * new_momentum, picked)
    return (loss, feat_grad, new_centers, new_momentum)
```

```python
import jax
import jax.numpy as jnp
from jax import lax
from jax.experimental import pallas as pl
from jax.experimental.pallas import tpu as pltpu
from jax.sharding import PartitionSpec as P

LOGIT_SCALE = 64.0
COS_MARGIN = 0.35
LEARN_RATE = 0.5
MOMENT_COEF = 0.9
DECAY_COEF = 0.0005
NORM_EPS = 1e-05
LENGTH_EPS = 1e-06
DEAD_MARK = 2.0

D = 512
FACE = 64
SAMP = 128
ROWS = 2048
NY, NZ, NK, NX = 4, 8, 2, 4
QUART = SAMP // NX
GROUP = FACE * NX
BOTH = GROUP * NK
BLOCK = QUART * NY
SLOTS = BLOCK * NZ
MESH = pl.DeviceIdType.MESH
F32 = jnp.float32
BF16 = jnp.bfloat16

NEAR_FIRST = (1, 7, 2, 6, 3, 5, 4)
FAR_FIRST = (4, 3, 5, 2, 6, 1, 7, 0)
XK = tuple((dx, dk) for dk in range(NK) for dx in range(NX) if dx or dk)


def nt_dot(a, b):
    return lax.dot_general(a, b, (((1,), (1,)), ((), ())), preferred_element_type=F32)


def tn_dot(a, b):
    return lax.dot_general(a, b, (((0,), (0,)), ((), ())), preferred_element_type=F32)


def normalize(values, gain):
    mean = jnp.sum(values, 0, keepdims=True) * (1.0 / GROUP)
    centered = values - mean
    spread = jnp.sum(centered * centered, 0, keepdims=True) * (1.0 / GROUP)
    return centered * (gain * lax.rsqrt(spread + NORM_EPS))


def kernel(
    faces_ref, w_first_ref, w_second_ref, gain_first_ref, bias_first_ref, gain_second_ref,
    centers_ref, momentum_ref, labels_ref, index_ref, live_ref,
    loss_ref, feat_ref, new_centers_ref, new_momentum_ref,
    face_buf, w1_buf, w2_buf, table, mtable, label_send, label_buf, pick, mpick,
    low_all, unit_rows, inv_len, unit_all, expo, weight_all,
    sum_send, sum_buf, raw_own, raw_send, y_buf, z_send, z_buf, grad_send, grad_buf, x_buf,
    local_sem, face_ss, face_rs, label_ss, label_rs, low_ss, low_rs, unit_ss, unit_rs,
    sum_ss, sum_rs, y_ss, y_rs, z_ss, z_rs, grad_ss, grad_rs, x_ss, x_rs,
):
    c = lax.axis_index("center")
    x = lax.axis_index("rep")
    y = c // (NZ * NK)
    z = lax.rem(c // NK, NZ)
    k = lax.rem(c, NK)

    def device(dx=0, dy=0, dz=0, dk=0):
        yy = lax.rem(y + dy % NY, NY)
        zz = lax.rem(z + dz % NZ, NZ)
        kk = lax.rem(k + dk % NK, NK)
        return ((yy * NZ + zz) * NK + kk, lax.rem(x + dx % NX, NX))

    def send(src, dst, ss, rs, dev):
        copy = pltpu.make_async_remote_copy(
            src_ref=src, dst_ref=dst, send_sem=ss, recv_sem=rs, device_id=dev, device_id_type=MESH
        )
        copy.start()
        return copy

    table_copy = pltpu.make_async_copy(centers_ref, table, local_sem.at[0])
    table_copy.start()
    my_face = face_buf.at[pl.ds(pl.multiple_of(x * FACE, FACE), FACE)]
    face_copy = pltpu.make_async_copy(faces_ref, my_face, local_sem.at[1])
    face_copy.start()
    w1_copy = pltpu.make_async_copy(w_first_ref, w1_buf, local_sem.at[2])
    w1_copy.start()
    w2_copy = pltpu.make_async_copy(w_second_ref, w2_buf, local_sem.at[3])
    w2_copy.start()
    mtable_copy = pltpu.make_async_copy(momentum_ref, mtable, local_sem.at[4])
    mtable_copy.start()

    barrier = pltpu.get_barrier_semaphore()
    peers = [dict(dx=dx, dk=dk) for dx, dk in XK]
    peers += [dict(dy=dy) for dy in range(1, NY)]
    peers += [dict(dz=dz) for dz in range(1, NZ)]
    for peer in peers:
        pl.semaphore_signal(barrier, inc=1, device_id=device(**peer), device_id_type=MESH)

    label_send[...] = jnp.zeros_like(label_send)
    label_send[:, 0:FACE] = labels_ref[...]
    first_row = pl.multiple_of(x * QUART, QUART)
    table_copy.wait()

    def take_center(i, carry):
        for j in range(8):
            row = first_row + i * 8 + j
            pick[pl.ds(row, 1), :] = table[pl.ds(index_ref[row], 1), :]
        return carry

    lax.fori_loop(0, QUART // 8, take_center, 0)
    mine = pick[pl.ds(first_row, QUART), :]
    mine_len = jnp.sqrt(jnp.sum(mine * mine, 1, keepdims=True) + LENGTH_EPS)
    row_id = lax.broadcasted_iota(jnp.int32, (QUART, D), 0) + first_row
    col_id = lax.broadcasted_iota(jnp.int32, (QUART, D), 1)
    mark = jnp.where(col_id == 0, DEAD_MARK, 0.0)
    low_all[0:QUART, :] = jnp.where(row_id < live_ref[0], mine / mine_len, mark).astype(BF16)

    pl.semaphore_wait(barrier, len(peers))

    copies = []
    face_copies = [
        send(faces_ref, my_face, face_ss.at[dx - 1], face_rs.at[dx - 1], device(dx=dx))
        for dx in (1, 3, 2)
    ]
    low_copies = {}

    def low_block(dy, dz):
        return low_all.at[pl.ds((dz * NY + dy) * QUART, QUART)]

    def send_low(dz_from, dy, dz):
        at = dz * NY + dy
        low_copies[dy, dz] = send(
            low_block(0, dz_from), low_block(dy, dz), low_ss.at[at], low_rs.at[at],
            device(dy=dy, dz=dz - dz_from),
        )

    for dz in NEAR_FIRST:
        send_low(0, 0, dz)
    for dy in (1, 3, 2):
        send_low(0, dy, 0)
    label_copies = [
        send(label_send, label_buf.at[i], label_ss.at[i], label_rs.at[i], device(dx=dx, dk=dk))
        for i, (dx, dk) in enumerate(XK)
    ]

    def forward(dz):
        low_copies[0, dz].wait_recv()
        for dy in (1, 3, 2):
            send_low(dz, dy, dz)

    w1_copy.wait()
    face_copy.wait()
    for copy in face_copies:
        copy.wait_recv()
    first_out = jnp.dot(face_buf[...], w1_buf[...], preferred_element_type=F32)
    hidden = jnp.maximum(
        normalize(first_out, gain_first_ref[...]) + bias_first_ref[...], 0.0
    ).astype(BF16)
    forward(1)
    forward(7)
    w2_copy.wait()
    second = jnp.dot(hidden, w2_buf[...], preferred_element_type=F32)
    feature = normalize(second, gain_second_ref[...])
    length = jnp.sqrt(jnp.sum(feature * feature, 1, keepdims=True) + LENGTH_EPS)
    inverse = 1.0 / length
    inv_len[...] = inverse
    unit = feature * inverse
    unit_rows[...] = unit
    unit_all[0:GROUP, :] = unit.astype(BF16)
    unit_copy = send(
        unit_all.at[pl.ds(0, GROUP)], unit_all.at[pl.ds(GROUP, GROUP)],
        unit_ss, unit_rs, device(dk=1),
    )
    for dz in (2, 6, 3, 5, 4):
        forward(dz)

    for copy in label_copies:
        copy.wait_recv()
    label_parts = {(0, 0): label_send[0:1, 0:FACE]}
    for i, (dx, dk) in enumerate(XK):
        label_parts[dx, dk] = label_buf[i, 0:1, 0:FACE]
    halves = []
    for dk in range(NK):
        pieces = []
        for at in range(NX):
            piece = label_parts[0, dk]
            for dx in range(1, NX):
                piece = jnp.where(lax.rem(x - at + NX, NX) == dx, label_parts[dx, dk], piece)
            pieces.append(piece)
        halves.append(jnp.concatenate(pieces, 1))
    marks = jnp.concatenate(halves, 1)

    def block_rows(dz):
        return pl.ds(dz * BLOCK, BLOCK)

    in_block = lax.broadcasted_iota(jnp.int32, (QUART, 1), 0)

    def slot_ids(dz):
        parts = []
        for dy in range(NY):
            yy = lax.rem(y - dy + NY, NY)
            zz = lax.rem(z - dz + NZ, NZ)
            parts.append(in_block + (((yy * NZ + zz) * NK + k) * SAMP + first_row))
        return jnp.concatenate(parts, 0)

    unit_copy.wait_recv()
    totals = jnp.zeros((1, BOTH), F32)
    targets = jnp.zeros((1, BOTH), F32)
    for dz in (0,) + NEAR_FIRST:
        for dy in range(1, NY):
            low_copies[dy, dz].wait_recv()
        low = low_all[block_rows(dz), :]
        live = low[:, 0:128].astype(F32)[:, 0:1] < 0.75 * DEAD_MARK
        hit = slot_ids(dz) == marks
        cosine = nt_dot(low, unit_all[...])
        logits = LOGIT_SCALE * jnp.where(hit, cosine - COS_MARGIN, cosine)
        exponent = jnp.exp(jnp.where(live, logits, -1e30))
        expo[block_rows(dz), :] = exponent
        totals += jnp.sum(exponent, 0, keepdims=True)
        targets += jnp.sum(jnp.where(hit, logits, 0.0), 0, keepdims=True)
    sum_send[0:1, :] = totals
    sum_send[1:2, :] = targets
    sum_copies = [
        send(sum_send, sum_buf.at[i], sum_ss.at[i], sum_rs.at[i], device(dx=dx, dk=dk))
        for i, (dx, dk) in enumerate(XK)
    ]

    mtable_copy.wait()

    def take_rest(i, carry):
        for j in range(8):
            row = i * 8 + j
            at = index_ref[row]
            pick[pl.ds(row, 1), :] = table[pl.ds(at, 1), :]
            mpick[pl.ds(row, 1), :] = mtable[pl.ds(at, 1), :]
        return carry

    lax.fori_loop(0, SAMP // 8, take_rest, 0)

    sums = sum_send[...]
    for (dx, dk), i, copy in zip(XK, range(len(XK)), sum_copies):
        copy.wait_recv()
        part = sum_buf[i]
        if dk:
            part = jnp.concatenate([part[:, GROUP:], part[:, :GROUP]], 1)
        sums = sums + part
    inverse_total = 1.0 / sums[0:1, :]
    face_loss = jnp.log(sums[0:1, :GROUP]) - sums[1:2, :GROUP]
    my_loss = face_loss[:, 0:FACE]
    for at in range(1, NX):
        my_loss = jnp.where(x == at, face_loss[:, at * FACE : (at + 1) * FACE], my_loss)
    loss_ref[...] = my_loss

    y_copies = {}
    for dz in FAR_FIRST:
        hit = slot_ids(dz) == marks
        share = expo[block_rows(dz), :] * inverse_total
        weight = (LOGIT_SCALE * jnp.where(hit, share - 1.0, share)).astype(BF16)
        weight_all[block_rows(dz), :] = weight
        raw = jnp.dot(weight, unit_all[...], preferred_element_type=F32)
        raw_own[pl.ds(dz * QUART, QUART), :] = raw[0:QUART, :]
        raw_send[pl.ds(dz * (BLOCK - QUART), BLOCK - QUART), :] = raw[QUART:, :].astype(BF16)
        for dy in (2, 1, 3):
            at = dz * (NY - 1) + dy - 1
            y_copies[dy, dz] = send(
                raw_send.at[pl.ds(at * QUART, QUART)], y_buf.at[pl.ds(at * QUART, QUART)],
                y_ss.at[at], y_rs.at[at], device(dy=-dy),
            )

    grad = tn_dot(weight_all[...], low_all[...])
    grad_send[...] = grad.astype(BF16)
    grad_copies = []
    for i, (dx, dk) in enumerate(XK):
        there = dk * GROUP + lax.rem(x + dx, NX) * FACE
        grad_copies.append(
            send(
                grad_send.at[pl.ds(pl.multiple_of(there, FACE), FACE)], grad_buf.at[i],
                grad_ss.at[i], grad_rs.at[i], device(dx=dx, dk=dk),
            )
        )
    my_grad = grad[0:FACE, :]
    for at in range(1, NX):
        my_grad = jnp.where(x == at, grad[at * FACE : (at + 1) * FACE, :], my_grad)

    z_copies = []
    for dz in FAR_FIRST:
        total = raw_own[pl.ds(dz * QUART, QUART), :]
        for dy in range(1, NY):
            y_copies[dy, dz].wait_recv()
        for dy in range(1, NY):
            at = dz * (NY - 1) + dy - 1
            total = total + y_buf[pl.ds(at * QUART, QUART), :].astype(F32)
        if dz:
            z_send[dz - 1] = total.astype(BF16)
            z_copies.append(
                send(z_send.at[dz - 1], z_buf.at[dz - 1], z_ss.at[dz - 1], z_rs.at[dz - 1], device(dz=-dz))
            )
        else:
            raw_mine = total

    for i, copy in enumerate(grad_copies):
        copy.wait_recv()
        my_grad = my_grad + grad_buf[i].astype(F32)
    my_unit = unit_rows[pl.ds(pl.multiple_of(x * FACE, FACE), FACE), :]
    my_inverse = inv_len[pl.ds(pl.multiple_of(x * FACE, FACE), FACE), :]
    radial = jnp.sum(my_unit * my_grad, 1, keepdims=True)
    feat_ref[...] = (my_grad - my_unit * radial) * my_inverse

    for copy in z_copies:
        copy.wait_recv()
    for i in range(NZ - 1):
        raw_mine = raw_mine + z_buf[i].astype(F32)
    x_slot = x_buf.at[pl.ds(first_row, QUART)]
    x_buf[pl.ds(first_row, QUART), :] = raw_mine.astype(BF16)
    x_copies = [
        send(x_slot, x_slot, x_ss.at[dx - 1], x_rs.at[dx - 1], device(dx=dx)) for dx in (2, 1, 3)
    ]
    picked = pick[...]
    center_inv = 1.0 / jnp.sqrt(jnp.sum(picked * picked, 1, keepdims=True) + LENGTH_EPS)
    center_unit = picked * center_inv
    held = mpick[...]
    drift = MOMENT_COEF * held + DECAY_COEF * picked
    slot_live = lax.broadcasted_iota(jnp.int32, (SAMP, 1), 0) < live_ref[0]
    for copy in x_copies:
        copy.wait_recv()
    raw_grad = x_buf[...].astype(F32)
    center_radial = jnp.sum(center_unit * raw_grad, 1, keepdims=True)
    velocity = drift + (raw_grad - center_unit * center_radial) * center_inv
    velocity = jnp.where(slot_live, velocity, held)
    new_momentum_ref[...] = velocity
    new_centers_ref[...] = jnp.where(slot_live, picked - LEARN_RATE * velocity, picked)

    copies = face_copies + label_copies + list(low_copies.values()) + [unit_copy] + sum_copies
    copies += list(y_copies.values()) + grad_copies + z_copies + x_copies
    for copy in copies:
        copy.wait_send()


def per_device(
    faces, w_first, w_second, gain_first, bias_first, gain_second,
    centers, momentum, sample_index, live_count, labels,
):
    vmem = pl.BlockSpec(memory_space=pltpu.VMEM)
    smem = pl.BlockSpec(memory_space=pltpu.SMEM)
    hbm = pl.BlockSpec(memory_space=pl.ANY)
    dma = pltpu.SemaphoreType.DMA
    peers = len(XK)
    loss, feat, new_centers, new_momentum = pl.pallas_call(
        kernel,
        out_shape=(
            jax.ShapeDtypeStruct((1, FACE), F32),
            jax.ShapeDtypeStruct((FACE, D), F32),
            jax.ShapeDtypeStruct((SAMP, D), F32),
            jax.ShapeDtypeStruct((SAMP, D), F32),
        ),
        in_specs=[hbm, hbm, hbm, vmem, vmem, vmem, hbm, hbm, vmem, smem, smem],
        out_specs=(vmem, vmem, vmem, vmem),
        scratch_shapes=[
            pltpu.VMEM((GROUP, D), BF16),
            pltpu.VMEM((D, D), BF16),
            pltpu.VMEM((D, D), BF16),
            pltpu.VMEM((ROWS, D), F32),
            pltpu.VMEM((ROWS, D), F32),
            pltpu.VMEM((1, 128), jnp.int32),
            pltpu.VMEM((peers, 1, 128), jnp.int32),
            pltpu.VMEM((SAMP, D), F32),
            pltpu.VMEM((SAMP, D), F32),
            pltpu.VMEM((SLOTS, D), BF16),
            pltpu.VMEM((GROUP, D), F32),
            pltpu.VMEM((GROUP, 1), F32),
            pltpu.VMEM((BOTH, D), BF16),
            pltpu.VMEM((SLOTS, BOTH), F32),
            pltpu.VMEM((SLOTS, BOTH), BF16),
            pltpu.VMEM((2, BOTH), F32),
            pltpu.VMEM((peers, 2, BOTH), F32),
            pltpu.VMEM((NZ * QUART, D), F32),
            pltpu.VMEM((NZ * (NY - 1) * QUART, D), BF16),
            pltpu.VMEM((NZ * (NY - 1) * QUART, D), BF16),
            pltpu.VMEM((NZ - 1, QUART, D), BF16),
            pltpu.VMEM((NZ - 1, QUART, D), BF16),
            pltpu.VMEM((BOTH, D), BF16),
            pltpu.VMEM((peers, FACE, D), BF16),
            pltpu.VMEM((SAMP, D), BF16),
            dma((5,)),
            dma((NX - 1,)), dma((NX - 1,)),
            dma((peers,)), dma((peers,)),
            dma((NZ * NY,)), dma((NZ * NY,)),
            dma, dma,
            dma((peers,)), dma((peers,)),
            dma((NZ * (NY - 1),)), dma((NZ * (NY - 1),)),
            dma((NZ - 1,)), dma((NZ - 1,)),
            dma((peers,)), dma((peers,)),
            dma((NX - 1,)), dma((NX - 1,)),
        ],
        compiler_params=pltpu.CompilerParams(
            collective_id=1, has_side_effects=True, vmem_limit_bytes=48 * 2**20
        ),
        name="margin_step",
    )(
        faces, w_first, w_second, gain_first.reshape(1, D), bias_first.reshape(1, D),
        gain_second.reshape(1, D), centers, momentum, labels.reshape(1, FACE),
        sample_index, live_count,
    )
    return loss.reshape(FACE), feat, new_centers, new_momentum


def solution(mesh):
    return jax.shard_map(
        per_device,
        mesh=mesh,
        in_specs=(
            P(("center", "rep"), None),
            P(), P(), P(), P(), P(),
            P("center", None),
            P("center", None),
            P("center"),
            P("center"),
            P(("center", "rep")),
        ),
        out_specs=(
            P(("center", "rep")),
            P(("center", "rep"), None),
            P("center", None),
            P("center", None),
        ),
        check_vma=False,
    )
```

```python
import jax
import jax.numpy as jnp
from jax import lax
from jax.experimental import pallas as pl
from jax.experimental.pallas import tpu as pltpu
from jax.sharding import PartitionSpec as P

LOGIT_SCALE = 64.0
COS_MARGIN = 0.35
LEARN_RATE = 0.5
MOMENT_COEF = 0.9
DECAY_COEF = 0.0005
NORM_EPS = 1e-05
LENGTH_EPS = 1e-06
DEAD_MARK = 2.0

D = 512
FACE = 64
SAMP = 128
ROWS = 2048
NY, NZ, NK, NX = 4, 8, 2, 4
QUART = SAMP // NX
HALF = D // 2
GROUP = FACE * NX
BOTH = GROUP * NK
BLOCK = QUART * NY
SLOTS = BLOCK * NZ
MESH = pl.DeviceIdType.MESH
F32 = jnp.float32
BF16 = jnp.bfloat16

NEAR_FIRST = (1, 7, 2, 6, 3, 5, 4)
ARRIVAL = (0,) + NEAR_FIRST
BESIDE = (1, 7)
BEYOND = (4, 3, 5, 2, 6)
LAG = 3
XK = tuple((dx, dk) for dk in range(NK) for dx in range(NX) if dx or dk)


def nt_dot(a, b):
    return lax.dot_general(a, b, (((1,), (1,)), ((), ())), preferred_element_type=F32)


def tn_dot(a, b):
    return lax.dot_general(a, b, (((0,), (0,)), ((), ())), preferred_element_type=F32)


def normalize(values, gain):
    mean = jnp.sum(values, 0, keepdims=True) * (1.0 / GROUP)
    centered = values - mean
    spread = jnp.sum(centered * centered, 0, keepdims=True) * (1.0 / GROUP)
    return centered * (gain * lax.rsqrt(spread + NORM_EPS))


def kernel(
    faces_ref, w_first_ref, w_second_ref, gain_first_hbm, bias_first_hbm, gain_second_hbm,
    centers_ref, momentum_ref, labels_hbm, index_hbm, live_ref,
    loss_ref, feat_ref, new_centers_ref, new_momentum_ref,
    gain_first_ref, bias_first_ref, gain_second_ref, labels_ref, index_ref,
    face_buf, w1_buf, w2_buf, table, mtable, label_send, label_buf, pick, mpick,
    low_all, unit_rows, inv_len, unit_all, expo, weight_all,
    sum_send, sum_buf, raw_here, side_send, side_buf, row_send, row_buf, raw_own, raw_next, near_send, near_buf, far_send, far_buf, z_send, z_buf, grad_send, grad_buf, x_buf,
    local_sem, face_ss, face_rs, label_ss, label_rs, low_ss, low_rs, half_ss, half_rs, unit_ss, unit_rs,
    sum_ss, sum_rs, side_ss, side_rs, row_ss, row_rs, near_ss, near_rs, far_ss, far_rs, z_ss, z_rs, grad_ss, grad_rs, x_ss, x_rs,
):
    c = lax.axis_index("center")
    x = lax.axis_index("rep")
    y = c // (NZ * NK)
    z = lax.rem(c // NK, NZ)
    k = lax.rem(c, NK)

    def device(dx=0, dy=0, dz=0, dk=0):
        yy = lax.rem(y + dy % NY, NY)
        zz = lax.rem(z + dz % NZ, NZ)
        kk = lax.rem(k + dk % NK, NK)
        return ((yy * NZ + zz) * NK + kk, lax.rem(x + dx % NX, NX))

    def send(src, dst, ss, rs, dev):
        copy = pltpu.make_async_remote_copy(
            src_ref=src, dst_ref=dst, send_sem=ss, recv_sem=rs, device_id=dev, device_id_type=MESH
        )
        copy.start()
        return copy

    my_face = face_buf.at[pl.ds(pl.multiple_of(x * FACE, FACE), FACE)]

    def load(i, src, dst):
        copy = pltpu.make_async_copy(src, dst, local_sem.at[i])
        copy.start()
        return copy

    table_copy = load(0, centers_ref, table)
    index_copy = load(1, index_hbm, index_ref)

    barrier = pltpu.get_barrier_semaphore()
    peers = [dict(dz=dz) for dz in reversed(NEAR_FIRST)]
    peers += [dict(dx=dx, dk=dk) for dx, dk in XK]
    peers += [dict(dy=dy) for dy in (2, 1, 3)]
    for peer in peers:
        pl.semaphore_signal(barrier, inc=1, device_id=device(**peer), device_id_type=MESH)

    label_copy = load(2, labels_hbm, labels_ref)
    face_copy = load(3, faces_ref, my_face)
    w1_copy = load(4, w_first_ref, w1_buf)
    gain_copies = [
        load(5, gain_first_hbm, gain_first_ref),
        load(6, bias_first_hbm, bias_first_ref),
        load(7, gain_second_hbm, gain_second_ref),
    ]
    w2_copy = load(8, w_second_ref, w2_buf)
    first_row = pl.multiple_of(x * QUART, QUART)

    index_copy.wait()
    table_copy.wait()

    def take_center(i, carry):
        for j in range(8):
            row = first_row + i * 8 + j
            pick[pl.ds(row, 1), :] = table[pl.ds(index_ref[row], 1), :]
        return carry

    lax.fori_loop(0, QUART // 8, take_center, 0)
    mine = pick[pl.ds(first_row, QUART), :]
    mine_len = jnp.sqrt(jnp.sum(mine * mine, 1, keepdims=True) + LENGTH_EPS)
    row_id = lax.broadcasted_iota(jnp.int32, (QUART, D), 0) + first_row
    col_id = lax.broadcasted_iota(jnp.int32, (QUART, D), 1)
    mark = jnp.where(col_id == 0, DEAD_MARK, 0.0)
    low_all[0:QUART, :] = jnp.where(row_id < live_ref[0], mine / mine_len, mark).astype(BF16)

    pl.semaphore_wait(barrier, len(peers))

    low_copies = {}

    def low_block(dy, dz):
        return low_all.at[pl.ds((dz * NY + dy) * QUART, QUART)]

    def send_low(dz_from, dy, dz, dy_from=0):
        at = dz * NY + dy
        low_copies[dy, dz] = send(
            low_block(dy_from, dz_from), low_block(dy, dz), low_ss.at[at], low_rs.at[at],
            device(dy=dy - dy_from, dz=dz - dz_from),
        )

    def sideways(dy):
        low_copies[dy, 0].wait_recv()
        for dz in BESIDE:
            send_low(0, dy, dz, dy)

    half_copies = {}

    def send_half(dz, part, dy_from):
        low_copies[dy_from, dz].wait_recv()
        rows = (dz * NY + dy_from) * QUART
        there = (dz * NY + 2) * QUART
        at = dz * 2 + part
        half_copies[part, dz] = send(
            low_all.at[pl.ds(rows, QUART), pl.ds(part * HALF, HALF)],
            low_all.at[pl.ds(there, QUART), pl.ds(part * HALF, HALF)],
            half_ss.at[at], half_rs.at[at], device(dy=dy_from),
        )

    def halves_on(dz):
        send_half(dz, 0, 1)
        send_half(dz, 1, NY - 1)

    for dz in (2, 6):
        send_low(0, 0, dz)
    for dy in (1, 3):
        send_low(0, dy, 0)
    face_copies = [
        send(faces_ref, my_face, face_ss.at[dx - 1], face_rs.at[dx - 1], device(dx=dx))
        for dx in (1, 3, 2)
    ]
    for dz in (3, 5, 4):
        send_low(0, 0, dz)
    send_low(0, 2, 0)
    for dz in BESIDE:
        send_low(0, 0, dz)

    def forward(dz):
        low_copies[0, dz].wait_recv()
        for dy in (1, 3, 2) if dz == NZ // 2 else (1, 3):
            send_low(dz, dy, dz)

    sideways(1)
    sideways(3)
    forward(2)
    forward(6)
    sideways(2)
    mtable_copy = load(9, momentum_ref, mtable)
    label_copy.wait()
    label_send[...] = jnp.zeros_like(label_send)
    label_send[:, 0:FACE] = labels_ref[...]
    label_copies = [
        send(label_send, label_buf.at[i], label_ss.at[i], label_rs.at[i], device(dx=dx, dk=dk))
        for i, (dx, dk) in enumerate(XK)
    ]


    for copy in gain_copies:
        copy.wait()
    w1_copy.wait()
    face_copy.wait()
    for copy in face_copies:
        copy.wait_recv()
    first_out = jnp.dot(face_buf[...], w1_buf[...], preferred_element_type=F32)
    hidden = jnp.maximum(
        normalize(first_out, gain_first_ref[...]) + bias_first_ref[...], 0.0
    ).astype(BF16)
    for dz in (3, 5, 4):
        forward(dz)
    w2_copy.wait()
    second = jnp.dot(hidden, w2_buf[...], preferred_element_type=F32)
    feature = normalize(second, gain_second_ref[...])
    length = jnp.sqrt(jnp.sum(feature * feature, 1, keepdims=True) + LENGTH_EPS)
    inverse = 1.0 / length
    inv_len[...] = inverse
    unit = feature * inverse
    unit_rows[...] = unit
    unit_all[0:GROUP, :] = unit.astype(BF16)
    unit_copy = send(
        unit_all.at[pl.ds(0, GROUP)], unit_all.at[pl.ds(GROUP, GROUP)],
        unit_ss, unit_rs, device(dk=1),
    )
    for dz in (2, 6, 3, 5):
        halves_on(dz)

    for copy in label_copies:
        copy.wait_recv()
    label_parts = {(0, 0): label_send[0:1, 0:FACE]}
    for i, (dx, dk) in enumerate(XK):
        label_parts[dx, dk] = label_buf[i, 0:1, 0:FACE]
    halves = []
    for dk in range(NK):
        pieces = []
        for at in range(NX):
            piece = label_parts[0, dk]
            for dx in range(1, NX):
                piece = jnp.where(lax.rem(x - at + NX, NX) == dx, label_parts[dx, dk], piece)
            pieces.append(piece)
        halves.append(jnp.concatenate(pieces, 1))
    marks = jnp.concatenate(halves, 1)

    def block_rows(dz):
        return pl.ds(dz * BLOCK, BLOCK)

    in_block = lax.broadcasted_iota(jnp.int32, (QUART, 1), 0)

    def slot_ids(dz):
        parts = []
        for dy in range(NY):
            yy = lax.rem(y - dy + NY, NY)
            zz = lax.rem(z - dz + NZ, NZ)
            parts.append(in_block + (((yy * NZ + zz) * NK + k) * SAMP + first_row))
        return jnp.concatenate(parts, 0)

    unit_copy.wait_recv()
    totals = jnp.zeros((1, BOTH), F32)
    targets = jnp.zeros((1, BOTH), F32)
    for step, dz in enumerate(ARRIVAL):
        if dz == 0:
            pass
        elif dz in BESIDE:
            for dy in range(NY):
                low_copies[dy, dz].wait_recv()
        elif dz == NZ // 2:
            for dy in range(1, NY):
                low_copies[dy, dz].wait_recv()
        else:
            for part in range(2):
                half_copies[part, dz].wait_recv()
        low = low_all[block_rows(dz), :]
        live = low[:, 0:128].astype(F32)[:, 0:1] < 0.75 * DEAD_MARK
        hit = slot_ids(dz) == marks
        cosine = nt_dot(low, unit_all[...])
        logits = LOGIT_SCALE * jnp.where(hit, cosine - COS_MARGIN, cosine)
        exponent = jnp.exp(jnp.where(live, logits, -1e30))
        expo[block_rows(dz), :] = exponent
        totals += jnp.sum(exponent, 0, keepdims=True)
        targets += jnp.sum(jnp.where(hit, logits, 0.0), 0, keepdims=True)
    sum_send[0:1, :] = totals
    sum_send[1:2, :] = targets
    sum_copies = [
        send(sum_send, sum_buf.at[i], sum_ss.at[i], sum_rs.at[i], device(dx=dx, dk=dk))
        for i, (dx, dk) in enumerate(XK)
    ]

    sums = sum_send[...]
    for (dx, dk), i, copy in zip(XK, range(len(XK)), sum_copies):
        copy.wait_recv()
        part = sum_buf[i]
        if dk:
            part = jnp.concatenate([part[:, GROUP:], part[:, :GROUP]], 1)
        sums = sums + part
    inverse_total = 1.0 / sums[0:1, :]
    face_loss = jnp.log(sums[0:1, :GROUP]) - sums[1:2, :GROUP]
    my_loss = face_loss[:, 0:FACE]
    for at in range(1, NX):
        my_loss = jnp.where(x == at, face_loss[:, at * FACE : (at + 1) * FACE], my_loss)
    loss_ref[...] = my_loss

    def raw_grad_of(dz):
        hit = slot_ids(dz) == marks
        share = expo[block_rows(dz), :] * inverse_total
        weight = (LOGIT_SCALE * jnp.where(hit, share - 1.0, share)).astype(BF16)
        weight_all[block_rows(dz), :] = weight
        return jnp.dot(weight, unit_all[...], preferred_element_type=F32)

    side_copies = []
    for i, dz in enumerate(BESIDE):
        side_send[i] = raw_grad_of(dz).astype(BF16)
        side_copies.append(
            send(side_send.at[i], side_buf.at[i], side_ss.at[i], side_rs.at[i], device(dz=-dz))
        )
    near_copies = {}
    for dz in BEYOND:
        raw = raw_grad_of(dz)
        part = [raw[dy * QUART : (dy + 1) * QUART, :] for dy in range(NY)]
        keep = pl.ds(dz * QUART, QUART)
        raw_own[keep, :] = part[0]
        raw_next[keep, 0:HALF] = part[1][:, 0:HALF]
        raw_next[keep, HALF:D] = part[3][:, HALF:D]
        near_send[2 * dz, :, 0:HALF] = part[2][:, 0:HALF].astype(BF16)
        near_send[2 * dz, :, HALF:D] = part[1][:, HALF:D].astype(BF16)
        near_send[2 * dz + 1, :, 0:HALF] = part[3][:, 0:HALF].astype(BF16)
        near_send[2 * dz + 1, :, HALF:D] = part[2][:, HALF:D].astype(BF16)
        for way, dy in enumerate((-1, 1)):
            at = 2 * dz + way
            near_copies[way, dz] = send(
                near_send.at[at], near_buf.at[at], near_ss.at[at], near_rs.at[at], device(dy=dy)
            )
    raw_here[...] = raw_grad_of(0)

    far_copies = {}
    z_copies = []

    def pass_on(dz):
        for way, dy in enumerate((-1, 1)):
            at = 2 * dz + way
            columns = pl.ds(way * HALF, HALF)
            near_copies[way, dz].wait_recv()
            passed = raw_next[pl.ds(dz * QUART, QUART), columns] + near_buf[at, :, columns].astype(F32)
            far_send[at] = passed.astype(BF16)
            far_copies[way, dz] = send(
                far_send.at[at], far_buf.at[at], far_ss.at[at], far_rs.at[at], device(dy=dy)
            )

    def gathered(dz):
        for way in range(2):
            far_copies[way, dz].wait_recv()
        left = near_buf[2 * dz + 1, :, 0:HALF].astype(F32) + far_buf[2 * dz].astype(F32)
        right = near_buf[2 * dz, :, HALF:D].astype(F32) + far_buf[2 * dz + 1].astype(F32)
        return raw_own[pl.ds(dz * QUART, QUART), :] + jnp.concatenate([left, right], 1)

    def send_on(dz):
        z_send[dz - 1] = gathered(dz).astype(BF16)
        z_copies.append(
            send(z_send.at[dz - 1], z_buf.at[dz - 1], z_ss.at[dz - 1], z_rs.at[dz - 1], device(dz=-dz))
        )

    grad = tn_dot(weight_all[...], low_all[...])
    grad_send[...] = grad.astype(BF16)
    grad_copies = []
    for i, (dx, dk) in enumerate(XK):
        there = dk * GROUP + lax.rem(x + dx, NX) * FACE
        grad_copies.append(
            send(
                grad_send.at[pl.ds(pl.multiple_of(there, FACE), FACE)], grad_buf.at[i],
                grad_ss.at[i], grad_rs.at[i], device(dx=dx, dk=dk),
            )
        )
    my_grad = grad[0:FACE, :]
    for at in range(1, NX):
        my_grad = jnp.where(x == at, grad[at * FACE : (at + 1) * FACE, :], my_grad)

    pass_on(BEYOND[0])
    pass_on(BEYOND[1])
    for copy in side_copies:
        copy.wait_recv()
    raw_mine = raw_here[0:QUART, :]
    for i in range(2):
        raw_mine = raw_mine + side_buf[i, 0:QUART, :].astype(F32)
    rest = raw_here[QUART:BLOCK, :]
    for i in range(2):
        rest = rest + side_buf[i, QUART:BLOCK, :].astype(F32)
    row_send[...] = rest.astype(BF16)
    row_copies = []
    for dy in (2, 1, 3):
        row_copies.append(
            send(
                row_send.at[pl.ds((dy - 1) * QUART, QUART)], row_buf.at[pl.ds((dy - 1) * QUART, QUART)],
                row_ss.at[dy - 1], row_rs.at[dy - 1], device(dy=-dy),
            )
        )
    for step in range(2, len(BEYOND) + LAG):
        if step < len(BEYOND):
            pass_on(BEYOND[step])
        if LAG <= step:
            send_on(BEYOND[step - LAG])

    mtable_copy.wait()

    def take_rest(i, carry):
        for j in range(8):
            row = i * 8 + j
            at = index_ref[row]
            pick[pl.ds(row, 1), :] = table[pl.ds(at, 1), :]
            mpick[pl.ds(row, 1), :] = mtable[pl.ds(at, 1), :]
        return carry

    lax.fori_loop(0, SAMP // 8, take_rest, 0)

    for i, copy in enumerate(grad_copies):
        copy.wait_recv()
        my_grad = my_grad + grad_buf[i].astype(F32)
    my_unit = unit_rows[pl.ds(pl.multiple_of(x * FACE, FACE), FACE), :]
    my_inverse = inv_len[pl.ds(pl.multiple_of(x * FACE, FACE), FACE), :]
    radial = jnp.sum(my_unit * my_grad, 1, keepdims=True)
    feat_ref[...] = (my_grad - my_unit * radial) * my_inverse

    for copy in row_copies:
        copy.wait_recv()
    for i in range(NY - 1):
        raw_mine = raw_mine + row_buf[pl.ds(i * QUART, QUART), :].astype(F32)
    for copy in z_copies:
        copy.wait_recv()
    for dz in BEYOND:
        raw_mine = raw_mine + z_buf[dz - 1].astype(F32)
    x_slot = x_buf.at[pl.ds(first_row, QUART)]
    x_buf[pl.ds(first_row, QUART), :] = raw_mine.astype(BF16)
    x_copies = [
        send(x_slot, x_slot, x_ss.at[dx - 1], x_rs.at[dx - 1], device(dx=dx)) for dx in (2, 1, 3)
    ]
    picked = pick[...]
    center_inv = 1.0 / jnp.sqrt(jnp.sum(picked * picked, 1, keepdims=True) + LENGTH_EPS)
    center_unit = picked * center_inv
    held = mpick[...]
    drift = MOMENT_COEF * held + DECAY_COEF * picked
    slot_live = lax.broadcasted_iota(jnp.int32, (SAMP, 1), 0) < live_ref[0]
    for copy in x_copies:
        copy.wait_recv()
    raw_grad = x_buf[...].astype(F32)
    center_radial = jnp.sum(center_unit * raw_grad, 1, keepdims=True)
    velocity = drift + (raw_grad - center_unit * center_radial) * center_inv
    velocity = jnp.where(slot_live, velocity, held)
    new_momentum_ref[...] = velocity
    new_centers_ref[...] = jnp.where(slot_live, picked - LEARN_RATE * velocity, picked)

    copies = face_copies + label_copies + list(low_copies.values()) + [unit_copy] + sum_copies
    copies += list(half_copies.values()) + list(near_copies.values()) + list(far_copies.values())
    copies += side_copies + row_copies
    copies += grad_copies + z_copies + x_copies
    for copy in copies:
        copy.wait_send()


def hand_over(*refs):
    sems = refs[8]
    copies = [pltpu.make_async_copy(refs[i], refs[i + 4], sems.at[i]) for i in range(4)]
    for copy in copies:
        copy.start()
    for copy in copies:
        copy.wait()


def per_device(
    faces, w_first, w_second, gain_first, bias_first, gain_second,
    centers, momentum, sample_index, live_count, labels,
):
    vmem = pl.BlockSpec(memory_space=pltpu.VMEM)
    smem = pl.BlockSpec(memory_space=pltpu.SMEM)
    hbm = pl.BlockSpec(memory_space=pltpu.HBM)
    dma = pltpu.SemaphoreType.DMA
    peers = len(XK)
    results = pl.pallas_call(
        kernel,
        out_shape=(
            jax.ShapeDtypeStruct((1, FACE), F32),
            jax.ShapeDtypeStruct((FACE, D), F32),
            jax.ShapeDtypeStruct((SAMP, D), F32),
            jax.ShapeDtypeStruct((SAMP, D), F32),
        ),
        in_specs=[hbm] * 10 + [smem],
        out_specs=(vmem, vmem, vmem, vmem),
        scratch_shapes=[
            pltpu.VMEM((1, D), F32),
            pltpu.VMEM((1, D), F32),
            pltpu.VMEM((1, D), F32),
            pltpu.VMEM((1, FACE), jnp.int32),
            pltpu.SMEM((SAMP,), jnp.int32),
            pltpu.VMEM((GROUP, D), BF16),
            pltpu.VMEM((D, D), BF16),
            pltpu.VMEM((D, D), BF16),
            pltpu.VMEM((ROWS, D), F32),
            pltpu.VMEM((ROWS, D), F32),
            pltpu.VMEM((1, 128), jnp.int32),
            pltpu.VMEM((peers, 1, 128), jnp.int32),
            pltpu.VMEM((SAMP, D), F32),
            pltpu.VMEM((SAMP, D), F32),
            pltpu.VMEM((SLOTS, D), BF16),
            pltpu.VMEM((GROUP, D), F32),
            pltpu.VMEM((GROUP, 1), F32),
            pltpu.VMEM((BOTH, D), BF16),
            pltpu.VMEM((SLOTS, BOTH), F32),
            pltpu.VMEM((SLOTS, BOTH), BF16),
            pltpu.VMEM((2, BOTH), F32),
            pltpu.VMEM((peers, 2, BOTH), F32),
            pltpu.VMEM((BLOCK, D), F32),
            pltpu.VMEM((2, BLOCK, D), BF16),
            pltpu.VMEM((2, BLOCK, D), BF16),
            pltpu.VMEM((BLOCK - QUART, D), BF16),
            pltpu.VMEM((BLOCK - QUART, D), BF16),
            pltpu.VMEM((NZ * QUART, D), F32),
            pltpu.VMEM((NZ * QUART, D), F32),
            pltpu.VMEM((2 * NZ, QUART, D), BF16),
            pltpu.VMEM((2 * NZ, QUART, D), BF16),
            pltpu.VMEM((2 * NZ, QUART, HALF), BF16),
            pltpu.VMEM((2 * NZ, QUART, HALF), BF16),
            pltpu.VMEM((NZ - 1, QUART, D), BF16),
            pltpu.VMEM((NZ - 1, QUART, D), BF16),
            pltpu.VMEM((BOTH, D), BF16),
            pltpu.VMEM((peers, FACE, D), BF16),
            pltpu.VMEM((SAMP, D), BF16),
            dma((10,)),
            dma((NX - 1,)), dma((NX - 1,)),
            dma((peers,)), dma((peers,)),
            dma((NZ * NY,)), dma((NZ * NY,)),
            dma((2 * NZ,)), dma((2 * NZ,)),
            dma, dma,
            dma((peers,)), dma((peers,)),
            dma((2,)), dma((2,)),
            dma((NY - 1,)), dma((NY - 1,)),
            dma((2 * NZ,)), dma((2 * NZ,)),
            dma((2 * NZ,)), dma((2 * NZ,)),
            dma((NZ - 1,)), dma((NZ - 1,)),
            dma((peers,)), dma((peers,)),
            dma((NX - 1,)), dma((NX - 1,)),
        ],
        compiler_params=pltpu.CompilerParams(
            collective_id=1, has_side_effects=True, vmem_limit_bytes=48 * 2**20
        ),
        name="margin_step",
    )(*[pltpu.with_memory_space_constraint(v, pltpu.HBM) for v in (
        faces, w_first, w_second, gain_first.reshape(1, D), bias_first.reshape(1, D),
        gain_second.reshape(1, D), centers, momentum, labels.reshape(1, FACE),
        sample_index)], live_count,
    )
    results = [pltpu.with_memory_space_constraint(r, pltpu.VMEM) for r in results]
    loss, feat, new_centers, new_momentum = pl.pallas_call(
        hand_over,
        out_shape=tuple(jax.ShapeDtypeStruct(r.shape, r.dtype) for r in results),
        in_specs=[pl.BlockSpec(memory_space=pltpu.VMEM)] * 4,
        out_specs=(pl.BlockSpec(memory_space=pl.ANY),) * 4,
        scratch_shapes=[dma((4,))],
        name="hand_over",
    )(*results)
    return loss.reshape(FACE), feat, new_centers, new_momentum


def solution(mesh):
    return jax.shard_map(
        per_device,
        mesh=mesh,
        in_specs=(
            P(("center", "rep"), None),
            P(), P(), P(), P(), P(),
            P("center", None),
            P("center", None),
            P("center"),
            P("center"),
            P(("center", "rep")),
        ),
        out_specs=(
            P(("center", "rep")),
            P(("center", "rep"), None),
            P("center", None),
            P("center", None),
        ),
        check_vma=False,
    )
```

```python
import jax
import jax.numpy as jnp
from jax import lax
from jax.experimental import pallas as pl
from jax.experimental.pallas import tpu as pltpu
from jax.sharding import PartitionSpec as P

LOGIT_SCALE = 64.0
COS_MARGIN = 0.35
LEARN_RATE = 0.5
MOMENT_COEF = 0.9
DECAY_COEF = 0.0005
NORM_EPS = 1e-05
LENGTH_EPS = 1e-06
DEAD_MARK = 2.0

D = 512
FACE = 64
SAMP = 128
ROWS = 2048
PIECE = 512
NY, NZ, NK, NX = 4, 8, 2, 4
QUART = SAMP // NX
GROUP = FACE * NX
BOTH = GROUP * NK
BLOCK = QUART * NY
SLOTS = BLOCK * NZ
MESH = pl.DeviceIdType.MESH
F32 = jnp.float32
BF16 = jnp.bfloat16

NEAR_FIRST = (1, 7, 2, 6, 3, 5, 4)
ARRIVAL = (0,) + NEAR_FIRST
BESIDE = (1, 7)
BEYOND = (4, 3, 5, 2, 6)
XK = tuple((dx, dk) for dk in range(NK) for dx in range(NX) if dx or dk)


def nt_dot(a, b):
    return lax.dot_general(a, b, (((1,), (1,)), ((), ())), preferred_element_type=F32)


def tn_dot(a, b):
    return lax.dot_general(a, b, (((0,), (0,)), ((), ())), preferred_element_type=F32)


def normalize(values, gain):
    mean = jnp.sum(values, 0, keepdims=True) * (1.0 / GROUP)
    centered = values - mean
    spread = jnp.sum(centered * centered, 0, keepdims=True) * (1.0 / GROUP)
    return centered * (gain * lax.rsqrt(spread + NORM_EPS))


def kernel(
    faces_ref, w_first_ref, w_second_ref, gain_first_hbm, bias_first_hbm, gain_second_hbm,
    centers_ref, momentum_ref, labels_hbm, index_hbm, live_ref,
    loss_ref, feat_ref, new_centers_ref, new_momentum_ref,
    gain_first_ref, bias_first_ref, gain_second_ref, labels_ref, index_ref,
    face_buf, w1_buf, w2_buf, table, mtable, label_send, label_buf, pick, mpick,
    low_all, unit_rows, inv_len, unit_all, expo, weight_all,
    sum_send, sum_buf, raw_here, side_send, side_buf, row_send, row_buf, raw_own, y_send, y_buf, z_send, z_buf, grad_send, grad_buf, x_buf,
    local_sem, face_ss, face_rs, label_ss, label_rs, low_ss, low_rs, unit_ss, unit_rs,
    sum_ss, sum_rs, side_ss, side_rs, row_ss, row_rs, y_ss, y_rs, z_ss, z_rs, grad_ss, grad_rs, x_ss, x_rs,
):
    c = lax.axis_index("center")
    x = lax.axis_index("rep")
    y = c // (NZ * NK)
    z = lax.rem(c // NK, NZ)
    k = lax.rem(c, NK)

    def device(dx=0, dy=0, dz=0, dk=0):
        yy = lax.rem(y + dy % NY, NY)
        zz = lax.rem(z + dz % NZ, NZ)
        kk = lax.rem(k + dk % NK, NK)
        return ((yy * NZ + zz) * NK + kk, lax.rem(x + dx % NX, NX))

    def send(src, dst, ss, rs, dev):
        copy = pltpu.make_async_remote_copy(
            src_ref=src, dst_ref=dst, send_sem=ss, recv_sem=rs, device_id=dev, device_id_type=MESH
        )
        copy.start()
        return copy

    my_face = face_buf.at[pl.ds(pl.multiple_of(x * FACE, FACE), FACE)]

    def load(i, src, dst):
        copy = pltpu.make_async_copy(src, dst, local_sem.at[i])
        copy.start()
        return copy

    table_copies = [
        load(9 + i, centers_ref.at[pl.ds(i * PIECE, PIECE)], table.at[pl.ds(i * PIECE, PIECE)])
        for i in range(ROWS // PIECE)
    ]
    index_copy = load(1, index_hbm, index_ref)

    barrier = pltpu.get_barrier_semaphore()
    peers = [dict(dz=dz) for dz in reversed(NEAR_FIRST)]
    peers += [dict(dx=dx, dk=dk) for dx, dk in XK]
    peers += [dict(dy=dy) for dy in (2, 1, 3)]
    for peer in peers:
        pl.semaphore_signal(barrier, inc=1, device_id=device(**peer), device_id_type=MESH)

    label_copy = load(2, labels_hbm, labels_ref)
    face_copy = load(3, faces_ref, my_face)
    w1_copy = load(4, w_first_ref, w1_buf)
    gain_copies = [
        load(5, gain_first_hbm, gain_first_ref),
        load(6, bias_first_hbm, bias_first_ref),
        load(7, gain_second_hbm, gain_second_ref),
    ]
    w2_copy = load(8, w_second_ref, w2_buf)
    first_row = pl.multiple_of(x * QUART, QUART)

    index_copy.wait()
    for copy in table_copies:
        copy.wait()

    def take_center(i, carry):
        for j in range(8):
            row = first_row + i * 8 + j
            pick[pl.ds(row, 1), :] = table[pl.ds(index_ref[row], 1), :]
        return carry

    lax.fori_loop(0, QUART // 8, take_center, 0)
    mine = pick[pl.ds(first_row, QUART), :]
    mine_len = jnp.sqrt(jnp.sum(mine * mine, 1, keepdims=True) + LENGTH_EPS)
    row_id = lax.broadcasted_iota(jnp.int32, (QUART, D), 0) + first_row
    col_id = lax.broadcasted_iota(jnp.int32, (QUART, D), 1)
    mark = jnp.where(col_id == 0, DEAD_MARK, 0.0)
    low_all[0:QUART, :] = jnp.where(row_id < live_ref[0], mine / mine_len, mark).astype(BF16)

    pl.semaphore_wait(barrier, len(peers))

    low_copies = {}

    def low_block(dy, dz):
        return low_all.at[pl.ds((dz * NY + dy) * QUART, QUART)]

    def send_low(dz_from, dy, dz, dy_from=0):
        at = dz * NY + dy
        low_copies[dy, dz] = send(
            low_block(dy_from, dz_from), low_block(dy, dz), low_ss.at[at], low_rs.at[at],
            device(dy=dy - dy_from, dz=dz - dz_from),
        )

    def sideways(dy):
        low_copies[dy, 0].wait_recv()
        for dz in BESIDE:
            send_low(0, dy, dz, dy)

    for dz in (2, 6):
        send_low(0, 0, dz)
    for dy in (1, 3):
        send_low(0, dy, 0)
    face_copies = [
        send(faces_ref, my_face, face_ss.at[dx - 1], face_rs.at[dx - 1], device(dx=dx))
        for dx in (1, 3, 2)
    ]
    for dz in (3, 5, 4):
        send_low(0, 0, dz)
    send_low(0, 2, 0)
    for dz in BESIDE:
        send_low(0, 0, dz)

    def forward(dz):
        low_copies[0, dz].wait_recv()
        for dy in (1, 3, 2):
            send_low(dz, dy, dz)

    sideways(1)
    sideways(3)
    forward(2)
    forward(6)
    sideways(2)
    mtable_copy = load(0, momentum_ref, mtable)
    label_copy.wait()
    label_send[...] = jnp.zeros_like(label_send)
    label_send[:, 0:FACE] = labels_ref[...]
    label_copies = [
        send(label_send, label_buf.at[i], label_ss.at[i], label_rs.at[i], device(dx=dx, dk=dk))
        for i, (dx, dk) in enumerate(XK)
    ]


    for copy in gain_copies:
        copy.wait()
    w1_copy.wait()
    face_copy.wait()
    for copy in face_copies:
        copy.wait_recv()
    first_out = jnp.dot(face_buf[...], w1_buf[...], preferred_element_type=F32)
    hidden = jnp.maximum(
        normalize(first_out, gain_first_ref[...]) + bias_first_ref[...], 0.0
    ).astype(BF16)
    for dz in (3, 5, 4):
        forward(dz)
    w2_copy.wait()
    second = jnp.dot(hidden, w2_buf[...], preferred_element_type=F32)
    feature = normalize(second, gain_second_ref[...])
    length = jnp.sqrt(jnp.sum(feature * feature, 1, keepdims=True) + LENGTH_EPS)
    inverse = 1.0 / length
    inv_len[...] = inverse
    unit = feature * inverse
    unit_rows[...] = unit
    unit_all[0:GROUP, :] = unit.astype(BF16)
    unit_copy = send(
        unit_all.at[pl.ds(0, GROUP)], unit_all.at[pl.ds(GROUP, GROUP)],
        unit_ss, unit_rs, device(dk=1),
    )
    for copy in label_copies:
        copy.wait_recv()
    label_parts = {(0, 0): label_send[0:1, 0:FACE]}
    for i, (dx, dk) in enumerate(XK):
        label_parts[dx, dk] = label_buf[i, 0:1, 0:FACE]
    halves = []
    for dk in range(NK):
        pieces = []
        for at in range(NX):
            piece = label_parts[0, dk]
            for dx in range(1, NX):
                piece = jnp.where(lax.rem(x - at + NX, NX) == dx, label_parts[dx, dk], piece)
            pieces.append(piece)
        halves.append(jnp.concatenate(pieces, 1))
    marks = jnp.concatenate(halves, 1)

    def block_rows(dz):
        return pl.ds(dz * BLOCK, BLOCK)

    in_block = lax.broadcasted_iota(jnp.int32, (QUART, 1), 0)

    def slot_ids(dz):
        parts = []
        for dy in range(NY):
            yy = lax.rem(y - dy + NY, NY)
            zz = lax.rem(z - dz + NZ, NZ)
            parts.append(in_block + (((yy * NZ + zz) * NK + k) * SAMP + first_row))
        return jnp.concatenate(parts, 0)

    unit_copy.wait_recv()
    totals = jnp.zeros((1, BOTH), F32)
    targets = jnp.zeros((1, BOTH), F32)
    for step, dz in enumerate(ARRIVAL):
        if dz == 0:
            pass
        elif dz in BESIDE:
            for dy in range(NY):
                low_copies[dy, dz].wait_recv()
        else:
            for dy in range(1, NY):
                low_copies[dy, dz].wait_recv()
        low = low_all[block_rows(dz), :]
        live = low[:, 0:128].astype(F32)[:, 0:1] < 0.75 * DEAD_MARK
        hit = slot_ids(dz) == marks
        cosine = nt_dot(low, unit_all[...])
        logits = LOGIT_SCALE * jnp.where(hit, cosine - COS_MARGIN, cosine)
        exponent = jnp.exp(jnp.where(live, logits, -1e30))
        expo[block_rows(dz), :] = exponent
        totals += jnp.sum(exponent, 0, keepdims=True)
        targets += jnp.sum(jnp.where(hit, logits, 0.0), 0, keepdims=True)
    sum_send[0:1, :] = totals
    sum_send[1:2, :] = targets
    sum_copies = [
        send(sum_send, sum_buf.at[i], sum_ss.at[i], sum_rs.at[i], device(dx=dx, dk=dk))
        for i, (dx, dk) in enumerate(XK)
    ]

    sums = sum_send[...]
    for (dx, dk), i, copy in zip(XK, range(len(XK)), sum_copies):
        copy.wait_recv()
        part = sum_buf[i]
        if dk:
            part = jnp.concatenate([part[:, GROUP:], part[:, :GROUP]], 1)
        sums = sums + part
    inverse_total = 1.0 / sums[0:1, :]
    face_loss = jnp.log(sums[0:1, :GROUP]) - sums[1:2, :GROUP]
    my_loss = face_loss[:, 0:FACE]
    for at in range(1, NX):
        my_loss = jnp.where(x == at, face_loss[:, at * FACE : (at + 1) * FACE], my_loss)
    loss_ref[...] = my_loss

    def raw_grad_of(dz):
        hit = slot_ids(dz) == marks
        share = expo[block_rows(dz), :] * inverse_total
        weight = (LOGIT_SCALE * jnp.where(hit, share - 1.0, share)).astype(BF16)
        weight_all[block_rows(dz), :] = weight
        return jnp.dot(weight, unit_all[...], preferred_element_type=F32)

    side_copies = []
    for i, dz in enumerate(BESIDE):
        side_send[i] = raw_grad_of(dz).astype(BF16)
        side_copies.append(
            send(side_send.at[i], side_buf.at[i], side_ss.at[i], side_rs.at[i], device(dz=-dz))
        )
    y_copies = {}
    for dz in BEYOND:
        raw = raw_grad_of(dz)
        raw_own[pl.ds(dz * QUART, QUART), :] = raw[0:QUART, :]
        y_send[pl.ds(dz * (BLOCK - QUART), BLOCK - QUART), :] = raw[QUART:BLOCK, :].astype(BF16)
        for dy in (2, 1, 3):
            at = dz * (NY - 1) + dy - 1
            y_copies[dy, dz] = send(
                y_send.at[pl.ds(at * QUART, QUART)], y_buf.at[pl.ds(at * QUART, QUART)],
                y_ss.at[at], y_rs.at[at], device(dy=-dy),
            )
    raw_here[...] = raw_grad_of(0)

    z_copies = []

    def gathered(dz):
        total = raw_own[pl.ds(dz * QUART, QUART), :]
        for dy in range(1, NY):
            y_copies[dy, dz].wait_recv()
        for dy in range(1, NY):
            at = dz * (NY - 1) + dy - 1
            total = total + y_buf[pl.ds(at * QUART, QUART), :].astype(F32)
        return total

    def send_on(dz):
        z_send[dz - 1] = gathered(dz).astype(BF16)
        z_copies.append(
            send(z_send.at[dz - 1], z_buf.at[dz - 1], z_ss.at[dz - 1], z_rs.at[dz - 1], device(dz=-dz))
        )

    grad = tn_dot(weight_all[...], low_all[...])
    grad_send[...] = grad.astype(BF16)
    grad_copies = []
    for i, (dx, dk) in enumerate(XK):
        there = dk * GROUP + lax.rem(x + dx, NX) * FACE
        grad_copies.append(
            send(
                grad_send.at[pl.ds(pl.multiple_of(there, FACE), FACE)], grad_buf.at[i],
                grad_ss.at[i], grad_rs.at[i], device(dx=dx, dk=dk),
            )
        )
    my_grad = grad[0:FACE, :]
    for at in range(1, NX):
        my_grad = jnp.where(x == at, grad[at * FACE : (at + 1) * FACE, :], my_grad)

    for copy in side_copies:
        copy.wait_recv()
    raw_mine = raw_here[0:QUART, :]
    for i in range(2):
        raw_mine = raw_mine + side_buf[i, 0:QUART, :].astype(F32)
    rest = raw_here[QUART:BLOCK, :]
    for i in range(2):
        rest = rest + side_buf[i, QUART:BLOCK, :].astype(F32)
    row_send[...] = rest.astype(BF16)
    row_copies = []
    for dy in (2, 1, 3):
        row_copies.append(
            send(
                row_send.at[pl.ds((dy - 1) * QUART, QUART)], row_buf.at[pl.ds((dy - 1) * QUART, QUART)],
                row_ss.at[dy - 1], row_rs.at[dy - 1], device(dy=-dy),
            )
        )
    for dz in BEYOND:
        send_on(dz)

    mtable_copy.wait()

    def take_rest(i, carry):
        for j in range(8):
            row = i * 8 + j
            at = index_ref[row]
            pick[pl.ds(row, 1), :] = table[pl.ds(at, 1), :]
            mpick[pl.ds(row, 1), :] = mtable[pl.ds(at, 1), :]
        return carry

    lax.fori_loop(0, SAMP // 8, take_rest, 0)

    for i, copy in enumerate(grad_copies):
        copy.wait_recv()
        my_grad = my_grad + grad_buf[i].astype(F32)
    my_unit = unit_rows[pl.ds(pl.multiple_of(x * FACE, FACE), FACE), :]
    my_inverse = inv_len[pl.ds(pl.multiple_of(x * FACE, FACE), FACE), :]
    radial = jnp.sum(my_unit * my_grad, 1, keepdims=True)
    feat_ref[...] = (my_grad - my_unit * radial) * my_inverse

    for copy in row_copies:
        copy.wait_recv()
    for i in range(NY - 1):
        raw_mine = raw_mine + row_buf[pl.ds(i * QUART, QUART), :].astype(F32)
    for copy in z_copies:
        copy.wait_recv()
    for dz in BEYOND:
        raw_mine = raw_mine + z_buf[dz - 1].astype(F32)
    x_slot = x_buf.at[pl.ds(first_row, QUART)]
    x_buf[pl.ds(first_row, QUART), :] = raw_mine.astype(BF16)
    x_copies = [
        send(x_slot, x_slot, x_ss.at[dx - 1], x_rs.at[dx - 1], device(dx=dx)) for dx in (2, 1, 3)
    ]
    picked = pick[...]
    center_inv = 1.0 / jnp.sqrt(jnp.sum(picked * picked, 1, keepdims=True) + LENGTH_EPS)
    center_unit = picked * center_inv
    held = mpick[...]
    drift = MOMENT_COEF * held + DECAY_COEF * picked
    slot_live = lax.broadcasted_iota(jnp.int32, (SAMP, 1), 0) < live_ref[0]
    for copy in x_copies:
        copy.wait_recv()
    raw_grad = x_buf[...].astype(F32)
    center_radial = jnp.sum(center_unit * raw_grad, 1, keepdims=True)
    velocity = drift + (raw_grad - center_unit * center_radial) * center_inv
    velocity = jnp.where(slot_live, velocity, held)
    new_momentum_ref[...] = velocity
    new_centers_ref[...] = jnp.where(slot_live, picked - LEARN_RATE * velocity, picked)

    copies = face_copies + label_copies + list(low_copies.values()) + [unit_copy] + sum_copies
    copies += list(y_copies.values())
    copies += side_copies + row_copies
    copies += grad_copies + z_copies + x_copies
    for copy in copies:
        copy.wait_send()


def hand_over(*refs):
    sems = refs[8]
    copies = [pltpu.make_async_copy(refs[i], refs[i + 4], sems.at[i]) for i in range(4)]
    for copy in copies:
        copy.start()
    for copy in copies:
        copy.wait()


def per_device(
    faces, w_first, w_second, gain_first, bias_first, gain_second,
    centers, momentum, sample_index, live_count, labels,
):
    vmem = pl.BlockSpec(memory_space=pltpu.VMEM)
    smem = pl.BlockSpec(memory_space=pltpu.SMEM)
    hbm = pl.BlockSpec(memory_space=pltpu.HBM)
    dma = pltpu.SemaphoreType.DMA
    peers = len(XK)
    results = pl.pallas_call(
        kernel,
        out_shape=(
            jax.ShapeDtypeStruct((1, FACE), F32),
            jax.ShapeDtypeStruct((FACE, D), F32),
            jax.ShapeDtypeStruct((SAMP, D), F32),
            jax.ShapeDtypeStruct((SAMP, D), F32),
        ),
        in_specs=[hbm] * 10 + [smem],
        out_specs=(vmem, vmem, vmem, vmem),
        scratch_shapes=[
            pltpu.VMEM((1, D), F32),
            pltpu.VMEM((1, D), F32),
            pltpu.VMEM((1, D), F32),
            pltpu.VMEM((1, FACE), jnp.int32),
            pltpu.SMEM((SAMP,), jnp.int32),
            pltpu.VMEM((GROUP, D), BF16),
            pltpu.VMEM((D, D), BF16),
            pltpu.VMEM((D, D), BF16),
            pltpu.VMEM((ROWS, D), F32),
            pltpu.VMEM((ROWS, D), F32),
            pltpu.VMEM((1, 128), jnp.int32),
            pltpu.VMEM((peers, 1, 128), jnp.int32),
            pltpu.VMEM((SAMP, D), F32),
            pltpu.VMEM((SAMP, D), F32),
            pltpu.VMEM((SLOTS, D), BF16),
            pltpu.VMEM((GROUP, D), F32),
            pltpu.VMEM((GROUP, 1), F32),
            pltpu.VMEM((BOTH, D), BF16),
            pltpu.VMEM((SLOTS, BOTH), F32),
            pltpu.VMEM((SLOTS, BOTH), BF16),
            pltpu.VMEM((2, BOTH), F32),
            pltpu.VMEM((peers, 2, BOTH), F32),
            pltpu.VMEM((BLOCK, D), F32),
            pltpu.VMEM((2, BLOCK, D), BF16),
            pltpu.VMEM((2, BLOCK, D), BF16),
            pltpu.VMEM((BLOCK - QUART, D), BF16),
            pltpu.VMEM((BLOCK - QUART, D), BF16),
            pltpu.VMEM((NZ * QUART, D), F32),
            pltpu.VMEM((NZ * (NY - 1) * QUART, D), BF16),
            pltpu.VMEM((NZ * (NY - 1) * QUART, D), BF16),
            pltpu.VMEM((NZ - 1, QUART, D), BF16),
            pltpu.VMEM((NZ - 1, QUART, D), BF16),
            pltpu.VMEM((BOTH, D), BF16),
            pltpu.VMEM((peers, FACE, D), BF16),
            pltpu.VMEM((SAMP, D), BF16),
            dma((13,)),
            dma((NX - 1,)), dma((NX - 1,)),
            dma((peers,)), dma((peers,)),
            dma((NZ * NY,)), dma((NZ * NY,)),
            dma, dma,
            dma((peers,)), dma((peers,)),
            dma((2,)), dma((2,)),
            dma((NY - 1,)), dma((NY - 1,)),
            dma((NZ * (NY - 1),)), dma((NZ * (NY - 1),)),
            dma((NZ - 1,)), dma((NZ - 1,)),
            dma((peers,)), dma((peers,)),
            dma((NX - 1,)), dma((NX - 1,)),
        ],
        compiler_params=pltpu.CompilerParams(
            collective_id=1, has_side_effects=True, vmem_limit_bytes=48 * 2**20
        ),
        name="margin_step",
    )(*[pltpu.with_memory_space_constraint(v, pltpu.HBM) for v in (
        faces, w_first, w_second, gain_first.reshape(1, D), bias_first.reshape(1, D),
        gain_second.reshape(1, D), centers, momentum, labels.reshape(1, FACE),
        sample_index)], live_count,
    )
    results = [pltpu.with_memory_space_constraint(r, pltpu.VMEM) for r in results]
    loss, feat, new_centers, new_momentum = pl.pallas_call(
        hand_over,
        out_shape=tuple(jax.ShapeDtypeStruct(r.shape, r.dtype) for r in results),
        in_specs=[pl.BlockSpec(memory_space=pltpu.VMEM)] * 4,
        out_specs=(pl.BlockSpec(memory_space=pl.ANY),) * 4,
        scratch_shapes=[dma((4,))],
        name="hand_over",
    )(*results)
    return loss.reshape(FACE), feat, new_centers, new_momentum


def solution(mesh):
    return jax.shard_map(
        per_device,
        mesh=mesh,
        in_specs=(
            P(("center", "rep"), None),
            P(), P(), P(), P(), P(),
            P("center", None),
            P("center", None),
            P("center"),
            P("center"),
            P(("center", "rep")),
        ),
        out_specs=(
            P(("center", "rep")),
            P(("center", "rep"), None),
            P("center", None),
            P("center", None),
        ),
        check_vma=False,
    )
```

```python
import jax
import jax.numpy as jnp
from jax import lax
from jax.experimental import pallas as pl
from jax.experimental.pallas import tpu as pltpu
from jax.sharding import PartitionSpec as P

LOGIT_SCALE = 64.0
COS_MARGIN = 0.35
LEARN_RATE = 0.5
MOMENT_COEF = 0.9
DECAY_COEF = 0.0005
NORM_EPS = 1e-05
LENGTH_EPS = 1e-06
DEAD_MARK = 2.0

D = 512
FACE = 64
SAMP = 128
ROWS = 2048
PIECE = 512
NY, NZ, NK, NX = 4, 8, 2, 4
QUART = SAMP // NX
GROUP = FACE * NX
BOTH = GROUP * NK
BLOCK = QUART * NY
SLOTS = BLOCK * NZ
MESH = pl.DeviceIdType.MESH
F32 = jnp.float32
BF16 = jnp.bfloat16

NEAR_FIRST = (1, 7, 2, 6, 3, 5, 4)
EARLY = (0, 1, 7, 2, 6)
LATE = (3, 5, 4)
BESIDE = (1, 7)
BEYOND = (4, 3, 5, 2, 6)
XK = tuple((dx, dk) for dk in range(NK) for dx in range(NX) if dx or dk)


def nt_dot(a, b):
    return lax.dot_general(a, b, (((1,), (1,)), ((), ())), preferred_element_type=F32)


def tn_dot(a, b):
    return lax.dot_general(a, b, (((0,), (0,)), ((), ())), preferred_element_type=F32)


def normalize(values, gain):
    mean = jnp.sum(values, 0, keepdims=True) * (1.0 / GROUP)
    centered = values - mean
    spread = jnp.sum(centered * centered, 0, keepdims=True) * (1.0 / GROUP)
    return centered * (gain * lax.rsqrt(spread + NORM_EPS))


def kernel(
    faces_ref, w_first_ref, w_second_ref, gain_first_hbm, bias_first_hbm, gain_second_hbm,
    centers_ref, momentum_ref, labels_hbm, index_hbm, live_hbm,
    loss_ref, feat_ref, new_centers_ref, new_momentum_ref,
    gain_first_ref, bias_first_ref, gain_second_ref, labels_ref, index_ref,
    face_buf, w1_buf, w2_buf, table, mtable, label_send, label_buf, pick, mpick,
    low_all, unit_rows, inv_len, unit_all, expo, weight_all,
    sum_send, sum_buf, raw_here, side_send, side_buf, row_send, row_buf, raw_own, y_send, y_buf, z_send, z_buf, grad_send, grad_buf, x_buf,
    local_sem, face_ss, face_rs, label_ss, label_rs, low_ss, low_rs, unit_ss, unit_rs,
    sum_ss, sum_rs, side_ss, side_rs, row_ss, row_rs, y_ss, y_rs, z_ss, z_rs, grad_ss, grad_rs, x_ss, x_rs,
):
    c = lax.axis_index("center")
    x = lax.axis_index("rep")
    y = c // (NZ * NK)
    z = lax.rem(c // NK, NZ)
    k = lax.rem(c, NK)

    def device(dx=0, dy=0, dz=0, dk=0):
        yy = lax.rem(y + dy % NY, NY)
        zz = lax.rem(z + dz % NZ, NZ)
        kk = lax.rem(k + dk % NK, NK)
        return ((yy * NZ + zz) * NK + kk, lax.rem(x + dx % NX, NX))

    def send(src, dst, ss, rs, dev):
        copy = pltpu.make_async_remote_copy(
            src_ref=src, dst_ref=dst, send_sem=ss, recv_sem=rs, device_id=dev, device_id_type=MESH
        )
        copy.start()
        return copy

    my_face = face_buf.at[pl.ds(pl.multiple_of(x * FACE, FACE), FACE)]

    def load(i, src, dst):
        copy = pltpu.make_async_copy(src, dst, local_sem.at[i])
        copy.start()
        return copy

    table_copies = [
        load(9 + i, centers_ref.at[pl.ds(i * PIECE, PIECE)], table.at[pl.ds(i * PIECE, PIECE)])
        for i in range(ROWS // PIECE)
    ]
    index_copy = load(1, index_hbm, index_ref)
    live_ref = live_hbm

    barrier = pltpu.get_barrier_semaphore()
    peers = [dict(dz=dz) for dz in reversed(NEAR_FIRST)]
    peers += [dict(dx=dx, dk=dk) for dx, dk in XK]
    peers += [dict(dy=dy) for dy in (2, 1, 3)]
    for peer in peers:
        pl.semaphore_signal(barrier, inc=1, device_id=device(**peer), device_id_type=MESH)

    label_copy = load(2, labels_hbm, labels_ref)
    face_copy = load(3, faces_ref, my_face)
    w1_copy = load(4, w_first_ref, w1_buf)
    gain_copies = [
        load(5, gain_first_hbm, gain_first_ref),
        load(6, bias_first_hbm, bias_first_ref),
        load(7, gain_second_hbm, gain_second_ref),
    ]
    w2_copy = load(8, w_second_ref, w2_buf)
    first_row = pl.multiple_of(x * QUART, QUART)

    index_copy.wait()
    for copy in table_copies:
        copy.wait()

    def take_center(i, carry):
        for j in range(8):
            row = first_row + i * 8 + j
            pick[pl.ds(row, 1), :] = table[pl.ds(index_ref[row], 1), :]
        return carry

    lax.fori_loop(0, QUART // 8, take_center, 0)
    mine = pick[pl.ds(first_row, QUART), :]
    mine_len = jnp.sqrt(jnp.sum(mine * mine, 1, keepdims=True) + LENGTH_EPS)
    row_id = lax.broadcasted_iota(jnp.int32, (QUART, D), 0) + first_row
    col_id = lax.broadcasted_iota(jnp.int32, (QUART, D), 1)
    mark = jnp.where(col_id == 0, DEAD_MARK, 0.0)
    low_all[0:QUART, :] = jnp.where(row_id < live_ref[0], mine / mine_len, mark).astype(BF16)

    pl.semaphore_wait(barrier, len(peers))

    face_copies = [
        send(faces_ref, my_face, face_ss.at[dx - 1], face_rs.at[dx - 1], device(dx=dx))
        for dx in (1, 3, 2)
    ]
    low_copies = {}

    def low_block(dy, dz):
        return low_all.at[pl.ds((dz * NY + dy) * QUART, QUART)]

    def send_low(dz_from, dy, dz, dy_from=0):
        at = dz * NY + dy
        low_copies[dy, dz] = send(
            low_block(dy_from, dz_from), low_block(dy, dz), low_ss.at[at], low_rs.at[at],
            device(dy=dy - dy_from, dz=dz - dz_from),
        )

    def sideways(dy):
        low_copies[dy, 0].wait_recv()
        for dz in BESIDE:
            send_low(0, dy, dz, dy)

    for dz in (2, 6):
        send_low(0, 0, dz)
    for dy in (1, 3):
        send_low(0, dy, 0)
    for dz in (3, 5, 4):
        send_low(0, 0, dz)
    send_low(0, 2, 0)
    for dz in BESIDE:
        send_low(0, 0, dz)

    def forward(dz):
        low_copies[0, dz].wait_recv()
        for dy in (1, 3, 2):
            send_low(dz, dy, dz)

    sideways(1)
    sideways(3)
    forward(2)
    forward(6)
    sideways(2)
    mtable_copy = load(0, momentum_ref, mtable)
    label_copy.wait()
    label_send[...] = jnp.zeros_like(label_send)
    label_send[:, 0:FACE] = labels_ref[...]
    label_copies = [
        send(label_send, label_buf.at[i], label_ss.at[i], label_rs.at[i], device(dx=dx, dk=dk))
        for i, (dx, dk) in enumerate(XK)
    ]


    for copy in gain_copies:
        copy.wait()
    w1_copy.wait()
    face_copy.wait()
    for copy in face_copies:
        copy.wait_recv()
    first_out = jnp.dot(face_buf[...], w1_buf[...], preferred_element_type=F32)
    hidden = jnp.maximum(
        normalize(first_out, gain_first_ref[...]) + bias_first_ref[...], 0.0
    ).astype(BF16)
    for dz in (3, 5):
        forward(dz)
    w2_copy.wait()
    second = jnp.dot(hidden, w2_buf[...], preferred_element_type=F32)
    feature = normalize(second, gain_second_ref[...])
    length = jnp.sqrt(jnp.sum(feature * feature, 1, keepdims=True) + LENGTH_EPS)
    inverse = 1.0 / length
    inv_len[...] = inverse
    unit = feature * inverse
    unit_rows[...] = unit
    unit_all[0:GROUP, :] = unit.astype(BF16)
    unit_copy = send(
        unit_all.at[pl.ds(0, GROUP)], unit_all.at[pl.ds(GROUP, GROUP)],
        unit_ss, unit_rs, device(dk=1),
    )
    forward(4)
    for copy in label_copies:
        copy.wait_recv()
    label_parts = {(0, 0): label_send[0:1, 0:FACE]}
    for i, (dx, dk) in enumerate(XK):
        label_parts[dx, dk] = label_buf[i, 0:1, 0:FACE]
    halves = []
    for dk in range(NK):
        pieces = []
        for at in range(NX):
            piece = label_parts[0, dk]
            for dx in range(1, NX):
                piece = jnp.where(lax.rem(x - at + NX, NX) == dx, label_parts[dx, dk], piece)
            pieces.append(piece)
        halves.append(jnp.concatenate(pieces, 1))
    marks = jnp.concatenate(halves, 1)

    def block_rows(dz):
        return pl.ds(dz * BLOCK, BLOCK)

    in_block = lax.broadcasted_iota(jnp.int32, (QUART, 1), 0)

    def slot_ids(dz):
        parts = []
        for dy in range(NY):
            yy = lax.rem(y - dy + NY, NY)
            zz = lax.rem(z - dz + NZ, NZ)
            parts.append(in_block + (((yy * NZ + zz) * NK + k) * SAMP + first_row))
        return jnp.concatenate(parts, 0)

    def await_block(dz):
        for dy in range(1 if dz not in BESIDE else 0, NY):
            low_copies[dy, dz].wait_recv()

    def score(dz, start, count):
        faces_here = pl.ds(start, count)
        low = low_all[block_rows(dz), :]
        live = low[:, 0:128].astype(F32)[:, 0:1] < 0.75 * DEAD_MARK
        hit = slot_ids(dz) == marks[:, start : start + count]
        cosine = nt_dot(low, unit_all[faces_here, :])
        logits = LOGIT_SCALE * jnp.where(hit, cosine - COS_MARGIN, cosine)
        exponent = jnp.exp(jnp.where(live, logits, -1e30))
        expo[block_rows(dz), faces_here] = exponent
        return (
            jnp.sum(exponent, 0, keepdims=True),
            jnp.sum(jnp.where(hit, logits, 0.0), 0, keepdims=True),
        )

    def add(a, b):
        return a[0] + b[0], a[1] + b[1]

    nothing = (jnp.zeros((1, GROUP), F32), jnp.zeros((1, GROUP), F32))
    own, other = nothing, nothing
    for dz in EARLY:
        if dz:
            await_block(dz)
        own = add(own, score(dz, 0, GROUP))
    unit_copy.wait_recv()
    for dz in EARLY:
        other = add(other, score(dz, GROUP, GROUP))
    both = (jnp.concatenate([own[0], other[0]], 1), jnp.concatenate([own[1], other[1]], 1))
    for dz in LATE:
        await_block(dz)
        both = add(both, score(dz, 0, BOTH))
    totals, targets = both
    sum_send[0:1, :] = totals
    sum_send[1:2, :] = targets
    sum_copies = [
        send(sum_send, sum_buf.at[i], sum_ss.at[i], sum_rs.at[i], device(dx=dx, dk=dk))
        for i, (dx, dk) in enumerate(XK)
    ]

    sums = sum_send[...]
    for (dx, dk), i, copy in zip(XK, range(len(XK)), sum_copies):
        copy.wait_recv()
        part = sum_buf[i]
        if dk:
            part = jnp.concatenate([part[:, GROUP:], part[:, :GROUP]], 1)
        sums = sums + part
    inverse_total = 1.0 / sums[0:1, :]
    def raw_grad_of(dz):
        hit = slot_ids(dz) == marks
        share = expo[block_rows(dz), :] * inverse_total
        weight = (LOGIT_SCALE * jnp.where(hit, share - 1.0, share)).astype(BF16)
        weight_all[block_rows(dz), :] = weight
        return jnp.dot(weight, unit_all[...], preferred_element_type=F32)

    side_copies = []
    for i, dz in enumerate(BESIDE):
        side_send[i] = raw_grad_of(dz).astype(BF16)
        side_copies.append(
            send(side_send.at[i], side_buf.at[i], side_ss.at[i], side_rs.at[i], device(dz=-dz))
        )
    y_copies = {}
    for dz in BEYOND:
        raw = raw_grad_of(dz)
        raw_own[pl.ds(dz * QUART, QUART), :] = raw[0:QUART, :]
        y_send[pl.ds(dz * (BLOCK - QUART), BLOCK - QUART), :] = raw[QUART:BLOCK, :].astype(BF16)
        for dy in (2, 1, 3):
            at = dz * (NY - 1) + dy - 1
            y_copies[dy, dz] = send(
                y_send.at[pl.ds(at * QUART, QUART)], y_buf.at[pl.ds(at * QUART, QUART)],
                y_ss.at[at], y_rs.at[at], device(dy=-dy),
            )
    raw_here[...] = raw_grad_of(0)

    face_loss = jnp.log(sums[0:1, :GROUP]) - sums[1:2, :GROUP]
    my_loss = face_loss[:, 0:FACE]
    for at in range(1, NX):
        my_loss = jnp.where(x == at, face_loss[:, at * FACE : (at + 1) * FACE], my_loss)
    loss_ref[...] = my_loss

    z_copies = []

    def gathered(dz):
        total = raw_own[pl.ds(dz * QUART, QUART), :]
        for dy in range(1, NY):
            y_copies[dy, dz].wait_recv()
        for dy in range(1, NY):
            at = dz * (NY - 1) + dy - 1
            total = total + y_buf[pl.ds(at * QUART, QUART), :].astype(F32)
        return total

    def send_on(dz):
        z_send[dz - 1] = gathered(dz).astype(BF16)
        z_copies.append(
            send(z_send.at[dz - 1], z_buf.at[dz - 1], z_ss.at[dz - 1], z_rs.at[dz - 1], device(dz=-dz))
        )

    grad = tn_dot(weight_all[...], low_all[...])
    grad_send[...] = grad.astype(BF16)
    grad_copies = []
    for i, (dx, dk) in enumerate(XK):
        there = dk * GROUP + lax.rem(x + dx, NX) * FACE
        grad_copies.append(
            send(
                grad_send.at[pl.ds(pl.multiple_of(there, FACE), FACE)], grad_buf.at[i],
                grad_ss.at[i], grad_rs.at[i], device(dx=dx, dk=dk),
            )
        )
    my_grad = grad[0:FACE, :]
    for at in range(1, NX):
        my_grad = jnp.where(x == at, grad[at * FACE : (at + 1) * FACE, :], my_grad)

    for copy in side_copies:
        copy.wait_recv()
    raw_mine = raw_here[0:QUART, :]
    for i in range(2):
        raw_mine = raw_mine + side_buf[i, 0:QUART, :].astype(F32)
    rest = raw_here[QUART:BLOCK, :]
    for i in range(2):
        rest = rest + side_buf[i, QUART:BLOCK, :].astype(F32)
    row_send[...] = rest.astype(BF16)
    row_copies = []
    for dy in (2, 1, 3):
        row_copies.append(
            send(
                row_send.at[pl.ds((dy - 1) * QUART, QUART)], row_buf.at[pl.ds((dy - 1) * QUART, QUART)],
                row_ss.at[dy - 1], row_rs.at[dy - 1], device(dy=-dy),
            )
        )
    for dz in BEYOND:
        send_on(dz)

    mtable_copy.wait()

    def take_rest(i, carry):
        for j in range(8):
            row = i * 8 + j
            at = index_ref[row]
            pick[pl.ds(row, 1), :] = table[pl.ds(at, 1), :]
            mpick[pl.ds(row, 1), :] = mtable[pl.ds(at, 1), :]
        return carry

    lax.fori_loop(0, SAMP // 8, take_rest, 0)

    for i, copy in enumerate(grad_copies):
        copy.wait_recv()
        my_grad = my_grad + grad_buf[i].astype(F32)
    my_unit = unit_rows[pl.ds(pl.multiple_of(x * FACE, FACE), FACE), :]
    my_inverse = inv_len[pl.ds(pl.multiple_of(x * FACE, FACE), FACE), :]
    radial = jnp.sum(my_unit * my_grad, 1, keepdims=True)
    feat_ref[...] = (my_grad - my_unit * radial) * my_inverse

    for copy in row_copies:
        copy.wait_recv()
    for i in range(NY - 1):
        raw_mine = raw_mine + row_buf[pl.ds(i * QUART, QUART), :].astype(F32)
    for copy in z_copies:
        copy.wait_recv()
    for dz in BEYOND:
        raw_mine = raw_mine + z_buf[dz - 1].astype(F32)
    x_slot = x_buf.at[pl.ds(first_row, QUART)]
    x_buf[pl.ds(first_row, QUART), :] = raw_mine.astype(BF16)
    x_copies = [
        send(x_slot, x_slot, x_ss.at[dx - 1], x_rs.at[dx - 1], device(dx=dx)) for dx in (2, 1, 3)
    ]
    picked = pick[...]
    center_inv = 1.0 / jnp.sqrt(jnp.sum(picked * picked, 1, keepdims=True) + LENGTH_EPS)
    center_unit = picked * center_inv
    held = mpick[...]
    drift = MOMENT_COEF * held + DECAY_COEF * picked
    slot_live = lax.broadcasted_iota(jnp.int32, (SAMP, 1), 0) < live_ref[0]
    for copy in x_copies:
        copy.wait_recv()
    raw_grad = x_buf[...].astype(F32)
    center_radial = jnp.sum(center_unit * raw_grad, 1, keepdims=True)
    velocity = drift + (raw_grad - center_unit * center_radial) * center_inv
    velocity = jnp.where(slot_live, velocity, held)
    new_momentum_ref[...] = velocity
    new_centers_ref[...] = jnp.where(slot_live, picked - LEARN_RATE * velocity, picked)

    copies = face_copies + label_copies + list(low_copies.values()) + [unit_copy] + sum_copies
    copies += list(y_copies.values())
    copies += side_copies + row_copies
    copies += grad_copies + z_copies + x_copies
    for copy in copies:
        copy.wait_send()


def hand_over(*refs):
    sems = refs[8]
    copies = [pltpu.make_async_copy(refs[i], refs[i + 4], sems.at[i]) for i in range(4)]
    for copy in copies:
        copy.start()
    for copy in copies:
        copy.wait()


def per_device(
    faces, w_first, w_second, gain_first, bias_first, gain_second,
    centers, momentum, sample_index, live_count, labels,
):
    vmem = pl.BlockSpec(memory_space=pltpu.VMEM)
    hbm = pl.BlockSpec(memory_space=pltpu.HBM)
    dma = pltpu.SemaphoreType.DMA
    peers = len(XK)
    results = pl.pallas_call(
        kernel,
        out_shape=(
            jax.ShapeDtypeStruct((1, FACE), F32),
            jax.ShapeDtypeStruct((FACE, D), F32),
            jax.ShapeDtypeStruct((SAMP, D), F32),
            jax.ShapeDtypeStruct((SAMP, D), F32),
        ),
        in_specs=[hbm] * 10 + [pl.BlockSpec(memory_space=pltpu.SMEM)],
        out_specs=(vmem, vmem, vmem, vmem),
        scratch_shapes=[
            pltpu.VMEM((1, D), F32),
            pltpu.VMEM((1, D), F32),
            pltpu.VMEM((1, D), F32),
            pltpu.VMEM((1, FACE), jnp.int32),
            pltpu.SMEM((SAMP,), jnp.int32),
            pltpu.VMEM((GROUP, D), BF16),
            pltpu.VMEM((D, D), BF16),
            pltpu.VMEM((D, D), BF16),
            pltpu.VMEM((ROWS, D), F32),
            pltpu.VMEM((ROWS, D), F32),
            pltpu.VMEM((1, 128), jnp.int32),
            pltpu.VMEM((peers, 1, 128), jnp.int32),
            pltpu.VMEM((SAMP, D), F32),
            pltpu.VMEM((SAMP, D), F32),
            pltpu.VMEM((SLOTS, D), BF16),
            pltpu.VMEM((GROUP, D), F32),
            pltpu.VMEM((GROUP, 1), F32),
            pltpu.VMEM((BOTH, D), BF16),
            pltpu.VMEM((SLOTS, BOTH), F32),
            pltpu.VMEM((SLOTS, BOTH), BF16),
            pltpu.VMEM((2, BOTH), F32),
            pltpu.VMEM((peers, 2, BOTH), F32),
            pltpu.VMEM((BLOCK, D), F32),
            pltpu.VMEM((2, BLOCK, D), BF16),
            pltpu.VMEM((2, BLOCK, D), BF16),
            pltpu.VMEM((BLOCK - QUART, D), BF16),
            pltpu.VMEM((BLOCK - QUART, D), BF16),
            pltpu.VMEM((NZ * QUART, D), F32),
            pltpu.VMEM((NZ * (NY - 1) * QUART, D), BF16),
            pltpu.VMEM((NZ * (NY - 1) * QUART, D), BF16),
            pltpu.VMEM((NZ - 1, QUART, D), BF16),
            pltpu.VMEM((NZ - 1, QUART, D), BF16),
            pltpu.VMEM((BOTH, D), BF16),
            pltpu.VMEM((peers, FACE, D), BF16),
            pltpu.VMEM((SAMP, D), BF16),
            dma((14,)),
            dma((NX - 1,)), dma((NX - 1,)),
            dma((peers,)), dma((peers,)),
            dma((NZ * NY,)), dma((NZ * NY,)),
            dma, dma,
            dma((peers,)), dma((peers,)),
            dma((2,)), dma((2,)),
            dma((NY - 1,)), dma((NY - 1,)),
            dma((NZ * (NY - 1),)), dma((NZ * (NY - 1),)),
            dma((NZ - 1,)), dma((NZ - 1,)),
            dma((peers,)), dma((peers,)),
            dma((NX - 1,)), dma((NX - 1,)),
        ],
        compiler_params=pltpu.CompilerParams(
            collective_id=1, has_side_effects=True, vmem_limit_bytes=48 * 2**20
        ),
        name="margin_step",
    )(*[pltpu.with_memory_space_constraint(v, pltpu.HBM) for v in (
        faces, w_first, w_second, gain_first.reshape(1, D), bias_first.reshape(1, D),
        gain_second.reshape(1, D), centers, momentum, labels.reshape(1, FACE),
        sample_index)], live_count,
    )
    results = [pltpu.with_memory_space_constraint(r, pltpu.VMEM) for r in results]
    loss, feat, new_centers, new_momentum = pl.pallas_call(
        hand_over,
        out_shape=tuple(jax.ShapeDtypeStruct(r.shape, r.dtype) for r in results),
        in_specs=[pl.BlockSpec(memory_space=pltpu.VMEM)] * 4,
        out_specs=(pl.BlockSpec(memory_space=pl.ANY),) * 4,
        scratch_shapes=[dma((4,))],
        name="hand_over",
    )(*results)
    return loss.reshape(FACE), feat, new_centers, new_momentum


def solution(mesh):
    return jax.shard_map(
        per_device,
        mesh=mesh,
        in_specs=(
            P(("center", "rep"), None),
            P(), P(), P(), P(), P(),
            P("center", None),
            P("center", None),
            P("center"),
            P("center"),
            P(("center", "rep")),
        ),
        out_specs=(
            P(("center", "rep")),
            P(("center", "rep"), None),
            P("center", None),
            P("center", None),
        ),
        check_vma=False,
    )
```

```python
import jax
import jax.numpy as jnp
from jax import lax
from jax.experimental import pallas as pl
from jax.experimental.pallas import tpu as pltpu
from jax.sharding import PartitionSpec as P

LOGIT_SCALE = 64.0
COS_MARGIN = 0.35
LEARN_RATE = 0.5
MOMENT_COEF = 0.9
DECAY_COEF = 0.0005
NORM_EPS = 1e-05
LENGTH_EPS = 1e-06
DEAD_MARK = 2.0

D = 512
FACE = 64
SAMP = 128
ROWS = 2048
PIECE = 512
NY, NZ, NK, NX = 4, 8, 2, 4
QUART = SAMP // NX
GROUP = FACE * NX
BOTH = GROUP * NK
BLOCK = QUART * NY
SLOTS = BLOCK * NZ
MESH = pl.DeviceIdType.MESH
F32 = jnp.float32
BF16 = jnp.bfloat16

NEAR_FIRST = (1, 7, 2, 6, 3, 5, 4)
EARLY = (0, 1, 7, 2, 6)
LATE = (3, 5, 4)
BESIDE = (1, 7)
BEYOND = (4, 3, 5, 2, 6)
XK = tuple((dx, dk) for dk in range(NK) for dx in range(NX) if dx or dk)


def nt_dot(a, b):
    return lax.dot_general(a, b, (((1,), (1,)), ((), ())), preferred_element_type=F32)


def tn_dot(a, b):
    return lax.dot_general(a, b, (((0,), (0,)), ((), ())), preferred_element_type=F32)


def normalize(values, gain):
    mean = jnp.sum(values, 0, keepdims=True) * (1.0 / GROUP)
    centered = values - mean
    spread = jnp.sum(centered * centered, 0, keepdims=True) * (1.0 / GROUP)
    return centered * (gain * lax.rsqrt(spread + NORM_EPS))


def kernel(
    faces_ref, w_first_ref, w_second_ref, gain_first_hbm, bias_first_hbm, gain_second_hbm,
    centers_ref, momentum_ref, labels_hbm, index_hbm, live_hbm,
    loss_ref, feat_ref, new_centers_ref, new_momentum_ref,
    gain_first_ref, bias_first_ref, gain_second_ref, labels_ref, index_ref,
    face_buf, w1_buf, w2_buf, table, mtable, label_send, label_buf, pick, mpick,
    low_all, unit_rows, inv_len, unit_all, expo, weight_all,
    sum_send, sum_buf, raw_here, side_send, side_buf, row_send, row_buf, raw_own, y_send, y_buf, z_send, z_buf, grad_send, grad_buf, x_buf,
    local_sem, face_ss, face_rs, label_ss, label_rs, low_ss, low_rs, unit_ss, unit_rs,
    sum_ss, sum_rs, side_ss, side_rs, row_ss, row_rs, y_ss, y_rs, z_ss, z_rs, grad_ss, grad_rs, x_ss, x_rs,
):
    c = lax.axis_index("center")
    x = lax.axis_index("rep")
    y = c // (NZ * NK)
    z = lax.rem(c // NK, NZ)
    k = lax.rem(c, NK)

    def device(dx=0, dy=0, dz=0, dk=0):
        yy = lax.rem(y + dy % NY, NY)
        zz = lax.rem(z + dz % NZ, NZ)
        kk = lax.rem(k + dk % NK, NK)
        return ((yy * NZ + zz) * NK + kk, lax.rem(x + dx % NX, NX))

    def send(src, dst, ss, rs, dev):
        copy = pltpu.make_async_remote_copy(
            src_ref=src, dst_ref=dst, send_sem=ss, recv_sem=rs, device_id=dev, device_id_type=MESH
        )
        copy.start()
        return copy

    my_face = face_buf.at[pl.ds(pl.multiple_of(x * FACE, FACE), FACE)]

    def load(i, src, dst):
        copy = pltpu.make_async_copy(src, dst, local_sem.at[i])
        copy.start()
        return copy

    table_copies = [
        load(9 + i, centers_ref.at[pl.ds(i * PIECE, PIECE)], table.at[pl.ds(i * PIECE, PIECE)])
        for i in range(ROWS // PIECE)
    ]
    index_copy = load(1, index_hbm, index_ref)
    live_ref = live_hbm

    barrier = pltpu.get_barrier_semaphore()
    peers = [dict(dz=dz) for dz in reversed(NEAR_FIRST)]
    peers += [dict(dx=dx, dk=dk) for dx, dk in XK]
    peers += [dict(dy=dy) for dy in (2, 1, 3)]
    for peer in peers:
        pl.semaphore_signal(barrier, inc=1, device_id=device(**peer), device_id_type=MESH)

    label_copy = load(2, labels_hbm, labels_ref)
    face_copy = load(3, faces_ref, my_face)
    w1_copy = load(4, w_first_ref, w1_buf)
    gain_copies = [
        load(5, gain_first_hbm, gain_first_ref),
        load(6, bias_first_hbm, bias_first_ref),
        load(7, gain_second_hbm, gain_second_ref),
    ]
    w2_copy = load(8, w_second_ref, w2_buf)
    first_row = pl.multiple_of(x * QUART, QUART)

    index_copy.wait()
    for copy in table_copies:
        copy.wait()

    def take_center(i, carry):
        for j in range(8):
            row = first_row + i * 8 + j
            pick[pl.ds(row, 1), :] = table[pl.ds(index_ref[row], 1), :]
        return carry

    lax.fori_loop(0, QUART // 8, take_center, 0)
    mine = pick[pl.ds(first_row, QUART), :]
    mine_len = jnp.sqrt(jnp.sum(mine * mine, 1, keepdims=True) + LENGTH_EPS)
    row_id = lax.broadcasted_iota(jnp.int32, (QUART, D), 0) + first_row
    col_id = lax.broadcasted_iota(jnp.int32, (QUART, D), 1)
    mark = jnp.where(col_id == 0, DEAD_MARK, 0.0)
    low_all[0:QUART, :] = jnp.where(row_id < live_ref[0], mine / mine_len, mark).astype(BF16)

    pl.semaphore_wait(barrier, len(peers))

    face_copies = [
        send(faces_ref, my_face, face_ss.at[dx - 1], face_rs.at[dx - 1], device(dx=dx))
        for dx in (1, 3, 2)
    ]
    low_copies = {}

    def low_block(dy, dz):
        return low_all.at[pl.ds((dz * NY + dy) * QUART, QUART)]

    def send_low(dz_from, dy, dz, dy_from=0):
        at = dz * NY + dy
        low_copies[dy, dz] = send(
            low_block(dy_from, dz_from), low_block(dy, dz), low_ss.at[at], low_rs.at[at],
            device(dy=dy - dy_from, dz=dz - dz_from),
        )

    def sideways(dy):
        low_copies[dy, 0].wait_recv()
        for dz in BESIDE:
            send_low(0, dy, dz, dy)

    for dz in (2, 6):
        send_low(0, 0, dz)
    for dy in (1, 3):
        send_low(0, dy, 0)
    for dz in (3, 5, 4):
        send_low(0, 0, dz)
    send_low(0, 2, 0)
    for dz in BESIDE:
        send_low(0, 0, dz)

    def forward(dz):
        low_copies[0, dz].wait_recv()
        for dy in (2, 1, 3):
            send_low(dz, dy, dz)

    sideways(1)
    sideways(3)
    forward(2)
    forward(6)
    sideways(2)
    mtable_copy = load(0, momentum_ref, mtable)
    label_copy.wait()
    label_send[...] = jnp.zeros_like(label_send)
    label_send[:, 0:FACE] = labels_ref[...]
    label_copies = [
        send(label_send, label_buf.at[i], label_ss.at[i], label_rs.at[i], device(dx=dx, dk=dk))
        for i, (dx, dk) in enumerate(XK)
    ]


    for copy in gain_copies:
        copy.wait()
    w1_copy.wait()
    face_copy.wait()
    for copy in face_copies:
        copy.wait_recv()
    first_out = jnp.dot(face_buf[...], w1_buf[...], preferred_element_type=F32)
    hidden = jnp.maximum(
        normalize(first_out, gain_first_ref[...]) + bias_first_ref[...], 0.0
    ).astype(BF16)
    for dz in (3, 5):
        forward(dz)
    w2_copy.wait()
    second = jnp.dot(hidden, w2_buf[...], preferred_element_type=F32)
    feature = normalize(second, gain_second_ref[...])
    length = jnp.sqrt(jnp.sum(feature * feature, 1, keepdims=True) + LENGTH_EPS)
    inverse = 1.0 / length
    inv_len[...] = inverse
    unit = feature * inverse
    unit_rows[...] = unit
    unit_all[0:GROUP, :] = unit.astype(BF16)
    unit_copy = send(
        unit_all.at[pl.ds(0, GROUP)], unit_all.at[pl.ds(GROUP, GROUP)],
        unit_ss, unit_rs, device(dk=1),
    )
    forward(4)
    for copy in label_copies:
        copy.wait_recv()
    label_parts = {(0, 0): label_send[0:1, 0:FACE]}
    for i, (dx, dk) in enumerate(XK):
        label_parts[dx, dk] = label_buf[i, 0:1, 0:FACE]
    halves = []
    for dk in range(NK):
        pieces = []
        for at in range(NX):
            piece = label_parts[0, dk]
            for dx in range(1, NX):
                piece = jnp.where(lax.rem(x - at + NX, NX) == dx, label_parts[dx, dk], piece)
            pieces.append(piece)
        halves.append(jnp.concatenate(pieces, 1))
    marks = jnp.concatenate(halves, 1)

    def block_rows(dz):
        return pl.ds(dz * BLOCK, BLOCK)

    in_block = lax.broadcasted_iota(jnp.int32, (QUART, 1), 0)

    def slot_ids(dz):
        parts = []
        for dy in range(NY):
            yy = lax.rem(y - dy + NY, NY)
            zz = lax.rem(z - dz + NZ, NZ)
            parts.append(in_block + (((yy * NZ + zz) * NK + k) * SAMP + first_row))
        return jnp.concatenate(parts, 0)

    def await_block(dz):
        for dy in range(1 if dz not in BESIDE else 0, NY):
            low_copies[dy, dz].wait_recv()

    def score(dz, start, count):
        faces_here = pl.ds(start, count)
        low = low_all[block_rows(dz), :]
        live = low[:, 0:128].astype(F32)[:, 0:1] < 0.75 * DEAD_MARK
        hit = slot_ids(dz) == marks[:, start : start + count]
        cosine = nt_dot(low, unit_all[faces_here, :])
        logits = LOGIT_SCALE * jnp.where(hit, cosine - COS_MARGIN, cosine)
        exponent = jnp.exp(jnp.where(live, logits, -1e30))
        expo[block_rows(dz), faces_here] = exponent
        return (
            jnp.sum(exponent, 0, keepdims=True),
            jnp.sum(jnp.where(hit, logits, 0.0), 0, keepdims=True),
        )

    def add(a, b):
        return a[0] + b[0], a[1] + b[1]

    nothing = (jnp.zeros((1, GROUP), F32), jnp.zeros((1, GROUP), F32))
    own, other = nothing, nothing
    for dz in EARLY:
        if dz:
            await_block(dz)
        own = add(own, score(dz, 0, GROUP))
    unit_copy.wait_recv()
    for dz in EARLY:
        other = add(other, score(dz, GROUP, GROUP))
    both = (jnp.concatenate([own[0], other[0]], 1), jnp.concatenate([own[1], other[1]], 1))
    for dz in LATE:
        await_block(dz)
        both = add(both, score(dz, 0, BOTH))
    totals, targets = both
    sum_send[0:1, :] = totals
    sum_send[1:2, :] = targets
    sum_copies = [
        send(sum_send, sum_buf.at[i], sum_ss.at[i], sum_rs.at[i], device(dx=dx, dk=dk))
        for i, (dx, dk) in enumerate(XK)
    ]

    sums = sum_send[...]
    for (dx, dk), i, copy in zip(XK, range(len(XK)), sum_copies):
        copy.wait_recv()
        part = sum_buf[i]
        if dk:
            part = jnp.concatenate([part[:, GROUP:], part[:, :GROUP]], 1)
        sums = sums + part
    inverse_total = 1.0 / sums[0:1, :]
    def raw_grad_of(dz):
        hit = slot_ids(dz) == marks
        share = expo[block_rows(dz), :] * inverse_total
        weight = (LOGIT_SCALE * jnp.where(hit, share - 1.0, share)).astype(BF16)
        weight_all[block_rows(dz), :] = weight
        return jnp.dot(weight, unit_all[...], preferred_element_type=F32)

    side_copies = []
    for i, dz in enumerate(BESIDE):
        side_send[i] = raw_grad_of(dz).astype(BF16)
        side_copies.append(
            send(side_send.at[i], side_buf.at[i], side_ss.at[i], side_rs.at[i], device(dz=-dz))
        )
    y_copies = {}
    for dz in BEYOND:
        raw = raw_grad_of(dz)
        raw_own[pl.ds(dz * QUART, QUART), :] = raw[0:QUART, :]
        y_send[pl.ds(dz * (BLOCK - QUART), BLOCK - QUART), :] = raw[QUART:BLOCK, :].astype(BF16)
        for dy in (2, 1, 3):
            at = dz * (NY - 1) + dy - 1
            y_copies[dy, dz] = send(
                y_send.at[pl.ds(at * QUART, QUART)], y_buf.at[pl.ds(at * QUART, QUART)],
                y_ss.at[at], y_rs.at[at], device(dy=-dy),
            )
    raw_here[...] = raw_grad_of(0)

    face_loss = jnp.log(sums[0:1, :GROUP]) - sums[1:2, :GROUP]
    my_loss = face_loss[:, 0:FACE]
    for at in range(1, NX):
        my_loss = jnp.where(x == at, face_loss[:, at * FACE : (at + 1) * FACE], my_loss)
    loss_ref[...] = my_loss

    z_copies = []

    def gathered(dz):
        total = raw_own[pl.ds(dz * QUART, QUART), :]
        for dy in range(1, NY):
            y_copies[dy, dz].wait_recv()
        for dy in range(1, NY):
            at = dz * (NY - 1) + dy - 1
            total = total + y_buf[pl.ds(at * QUART, QUART), :].astype(F32)
        return total

    def send_on(dz):
        z_send[dz - 1] = gathered(dz).astype(BF16)
        z_copies.append(
            send(z_send.at[dz - 1], z_buf.at[dz - 1], z_ss.at[dz - 1], z_rs.at[dz - 1], device(dz=-dz))
        )

    grad = tn_dot(weight_all[...], low_all[...])
    grad_send[...] = grad.astype(BF16)
    grad_copies = []
    for i, (dx, dk) in enumerate(XK):
        there = dk * GROUP + lax.rem(x + dx, NX) * FACE
        grad_copies.append(
            send(
                grad_send.at[pl.ds(pl.multiple_of(there, FACE), FACE)], grad_buf.at[i],
                grad_ss.at[i], grad_rs.at[i], device(dx=dx, dk=dk),
            )
        )
    my_grad = grad[0:FACE, :]
    for at in range(1, NX):
        my_grad = jnp.where(x == at, grad[at * FACE : (at + 1) * FACE, :], my_grad)

    for copy in side_copies:
        copy.wait_recv()
    raw_mine = raw_here[0:QUART, :]
    for i in range(2):
        raw_mine = raw_mine + side_buf[i, 0:QUART, :].astype(F32)
    rest = raw_here[QUART:BLOCK, :]
    for i in range(2):
        rest = rest + side_buf[i, QUART:BLOCK, :].astype(F32)
    row_send[...] = rest.astype(BF16)
    row_copies = []
    for dy in (2, 1, 3):
        row_copies.append(
            send(
                row_send.at[pl.ds((dy - 1) * QUART, QUART)], row_buf.at[pl.ds((dy - 1) * QUART, QUART)],
                row_ss.at[dy - 1], row_rs.at[dy - 1], device(dy=-dy),
            )
        )
    for dz in BEYOND:
        send_on(dz)

    mtable_copy.wait()

    def take_rest(i, carry):
        for j in range(8):
            row = i * 8 + j
            at = index_ref[row]
            pick[pl.ds(row, 1), :] = table[pl.ds(at, 1), :]
            mpick[pl.ds(row, 1), :] = mtable[pl.ds(at, 1), :]
        return carry

    lax.fori_loop(0, SAMP // 8, take_rest, 0)

    for i, copy in enumerate(grad_copies):
        copy.wait_recv()
        my_grad = my_grad + grad_buf[i].astype(F32)
    my_unit = unit_rows[pl.ds(pl.multiple_of(x * FACE, FACE), FACE), :]
    my_inverse = inv_len[pl.ds(pl.multiple_of(x * FACE, FACE), FACE), :]
    radial = jnp.sum(my_unit * my_grad, 1, keepdims=True)
    feat_ref[...] = (my_grad - my_unit * radial) * my_inverse

    for copy in row_copies:
        copy.wait_recv()
    for i in range(NY - 1):
        raw_mine = raw_mine + row_buf[pl.ds(i * QUART, QUART), :].astype(F32)
    for copy in z_copies:
        copy.wait_recv()
    for dz in BEYOND:
        raw_mine = raw_mine + z_buf[dz - 1].astype(F32)
    x_slot = x_buf.at[pl.ds(first_row, QUART)]
    x_buf[pl.ds(first_row, QUART), :] = raw_mine.astype(BF16)
    x_copies = [
        send(x_slot, x_slot, x_ss.at[dx - 1], x_rs.at[dx - 1], device(dx=dx)) for dx in (2, 1, 3)
    ]
    picked = pick[...]
    center_inv = 1.0 / jnp.sqrt(jnp.sum(picked * picked, 1, keepdims=True) + LENGTH_EPS)
    center_unit = picked * center_inv
    held = mpick[...]
    drift = MOMENT_COEF * held + DECAY_COEF * picked
    slot_live = lax.broadcasted_iota(jnp.int32, (SAMP, 1), 0) < live_ref[0]
    for copy in x_copies:
        copy.wait_recv()
    raw_grad = x_buf[...].astype(F32)
    center_radial = jnp.sum(center_unit * raw_grad, 1, keepdims=True)
    velocity = drift + (raw_grad - center_unit * center_radial) * center_inv
    velocity = jnp.where(slot_live, velocity, held)
    new_momentum_ref[...] = velocity
    new_centers_ref[...] = jnp.where(slot_live, picked - LEARN_RATE * velocity, picked)

    copies = face_copies + label_copies + list(low_copies.values()) + [unit_copy] + sum_copies
    copies += list(y_copies.values())
    copies += side_copies + row_copies
    copies += grad_copies + z_copies + x_copies
    for copy in copies:
        copy.wait_send()


def hand_over(*refs):
    sems = refs[8]
    copies = [pltpu.make_async_copy(refs[i], refs[i + 4], sems.at[i]) for i in range(4)]
    for copy in copies:
        copy.start()
    for copy in copies:
        copy.wait()


def per_device(
    faces, w_first, w_second, gain_first, bias_first, gain_second,
    centers, momentum, sample_index, live_count, labels,
):
    vmem = pl.BlockSpec(memory_space=pltpu.VMEM)
    hbm = pl.BlockSpec(memory_space=pltpu.HBM)
    dma = pltpu.SemaphoreType.DMA
    peers = len(XK)
    results = pl.pallas_call(
        kernel,
        out_shape=(
            jax.ShapeDtypeStruct((1, FACE), F32),
            jax.ShapeDtypeStruct((FACE, D), F32),
            jax.ShapeDtypeStruct((SAMP, D), F32),
            jax.ShapeDtypeStruct((SAMP, D), F32),
        ),
        in_specs=[hbm] * 10 + [pl.BlockSpec(memory_space=pltpu.SMEM)],
        out_specs=(vmem, vmem, vmem, vmem),
        scratch_shapes=[
            pltpu.VMEM((1, D), F32),
            pltpu.VMEM((1, D), F32),
            pltpu.VMEM((1, D), F32),
            pltpu.VMEM((1, FACE), jnp.int32),
            pltpu.SMEM((SAMP,), jnp.int32),
            pltpu.VMEM((GROUP, D), BF16),
            pltpu.VMEM((D, D), BF16),
            pltpu.VMEM((D, D), BF16),
            pltpu.VMEM((ROWS, D), F32),
            pltpu.VMEM((ROWS, D), F32),
            pltpu.VMEM((1, 128), jnp.int32),
            pltpu.VMEM((peers, 1, 128), jnp.int32),
            pltpu.VMEM((SAMP, D), F32),
            pltpu.VMEM((SAMP, D), F32),
            pltpu.VMEM((SLOTS, D), BF16),
            pltpu.VMEM((GROUP, D), F32),
            pltpu.VMEM((GROUP, 1), F32),
            pltpu.VMEM((BOTH, D), BF16),
            pltpu.VMEM((SLOTS, BOTH), F32),
            pltpu.VMEM((SLOTS, BOTH), BF16),
            pltpu.VMEM((2, BOTH), F32),
            pltpu.VMEM((peers, 2, BOTH), F32),
            pltpu.VMEM((BLOCK, D), F32),
            pltpu.VMEM((2, BLOCK, D), BF16),
            pltpu.VMEM((2, BLOCK, D), BF16),
            pltpu.VMEM((BLOCK - QUART, D), BF16),
            pltpu.VMEM((BLOCK - QUART, D), BF16),
            pltpu.VMEM((NZ * QUART, D), F32),
            pltpu.VMEM((NZ * (NY - 1) * QUART, D), BF16),
            pltpu.VMEM((NZ * (NY - 1) * QUART, D), BF16),
            pltpu.VMEM((NZ - 1, QUART, D), BF16),
            pltpu.VMEM((NZ - 1, QUART, D), BF16),
            pltpu.VMEM((BOTH, D), BF16),
            pltpu.VMEM((peers, FACE, D), BF16),
            pltpu.VMEM((SAMP, D), BF16),
            dma((14,)),
            dma((NX - 1,)), dma((NX - 1,)),
            dma((peers,)), dma((peers,)),
            dma((NZ * NY,)), dma((NZ * NY,)),
            dma, dma,
            dma((peers,)), dma((peers,)),
            dma((2,)), dma((2,)),
            dma((NY - 1,)), dma((NY - 1,)),
            dma((NZ * (NY - 1),)), dma((NZ * (NY - 1),)),
            dma((NZ - 1,)), dma((NZ - 1,)),
            dma((peers,)), dma((peers,)),
            dma((NX - 1,)), dma((NX - 1,)),
        ],
        compiler_params=pltpu.CompilerParams(
            collective_id=1, has_side_effects=True, vmem_limit_bytes=48 * 2**20
        ),
        name="margin_step",
    )(*[pltpu.with_memory_space_constraint(v, pltpu.HBM) for v in (
        faces, w_first, w_second, gain_first.reshape(1, D), bias_first.reshape(1, D),
        gain_second.reshape(1, D), centers, momentum, labels.reshape(1, FACE),
        sample_index)], live_count,
    )
    results = [pltpu.with_memory_space_constraint(r, pltpu.VMEM) for r in results]
    loss, feat, new_centers, new_momentum = pl.pallas_call(
        hand_over,
        out_shape=tuple(jax.ShapeDtypeStruct(r.shape, r.dtype) for r in results),
        in_specs=[pl.BlockSpec(memory_space=pltpu.VMEM)] * 4,
        out_specs=(pl.BlockSpec(memory_space=pl.ANY),) * 4,
        scratch_shapes=[dma((4,))],
        name="hand_over",
    )(*results)
    return loss.reshape(FACE), feat, new_centers, new_momentum


def solution(mesh):
    return jax.shard_map(
        per_device,
        mesh=mesh,
        in_specs=(
            P(("center", "rep"), None),
            P(), P(), P(), P(), P(),
            P("center", None),
            P("center", None),
            P("center"),
            P("center"),
            P(("center", "rep")),
        ),
        out_specs=(
            P(("center", "rep")),
            P(("center", "rep"), None),
            P("center", None),
            P("center", None),
        ),
        check_vma=False,
    )
```
